32 devices in a mesh: shot: 8 (over z, y), dom: 4 (over x, core).
Axes of the slice: x: 2, y: 2, z: 4, core: 2. Of those that a mesh axis runs over, the one named last changes fastest.
Arguments:
- coefficient: float32 [128, 16, 384], P('dom'), may hold values from 0.02 to 0.18
- fwd_older: float32 [8, 128, 16, 384], P('shot', 'dom'), may hold values from -6 to 6
- fwd_recent: float32 [8, 128, 16, 384], P('shot', 'dom'), may hold values from -6 to 6
- adj_later: float32 [8, 128, 16, 384], P('shot', 'dom'), may hold values from -6 to 6
- adj_recent: float32 [8, 128, 16, 384], P('shot', 'dom'), may hold values from -6 to 6
- source_xcell: int32 [8], P('shot'), may hold values from 0 to 127
- source_ycell: int32 [8], P('shot'), may hold values from 0 to 15
- source_zcell: int32 [8], P('shot'), may hold values from 0 to 383
- amplitude: float32 [8, 2], P('shot'), may hold values from 1773.62 to 3547.24
- receiver_xcell: int32 [8, 1024], P('shot'), may hold values from 0 to 127
- receiver_ycell: int32 [8, 1024], P('shot'), may hold values from 0 to 15
- receiver_zcell: int32 [8, 1024], P('shot'), may hold values from 0 to 383
- observed: float32 [8, 2, 1024], P('shot'), may hold values from -6 to 6
Outputs:
- fwd_latest: float32 [8, 128, 16, 384], P('shot', 'dom')
- adj_latest: float32 [8, 128, 16, 384], P('shot', 'dom')
- model_gradient: float32 [128, 16, 384], P('dom')
The draws below stay inside these ranges and needn't reach their ends.
All inputs are finite; a program needn't handle non-finite values.
Results may differ from the reference program's by a relative error of at most 0.0003.
Values sent between devices are 32-bit elements; how exact they have to be, the bound alone decides.
A program may use at most 64 MiB of HBM per device.

```python
import math
import jax
import jax.numpy as jnp
from jax import lax

R = 4
NY = 16
NZ = 384
RECV = 1024
NX = 128
SHOTS = 8


def with_ends(drawn, rng, smallest, top_value):
    shape = drawn.shape
    place = [jax.random.randint(jax.random.fold_in(rng, axis), (), 0, shape[axis]) for axis in range(len(shape))]
    drawn = drawn.at[tuple(place)].set(smallest)
    longest = shape.index(max(shape))
    place[longest] = (place[longest] + 1) % shape[longest]
    return drawn.at[tuple(place)].set(top_value)


def level_of(own_key, dims, cuts, smallest, high):
    gain = 1.0
    for position, blocks in cuts:
        steps = jax.random.uniform(jax.random.fold_in(jax.random.fold_in(own_key, 6), position), (blocks,), jnp.float32, smallest / len(cuts), high / len(cuts))
        gain = gain * jnp.repeat(jnp.exp(steps), dims[position] // blocks).reshape((-1,) + (1,) * (len(dims) - 1 - position))
    return gain


def noise(stream_key, shape, spread, limit, pieces=(), kind=jnp.bfloat16):
    level = level_of(stream_key, shape, pieces, -0.22, 0.18) if pieces else 1.0
    result = jax.random.normal(stream_key, shape, jnp.float32) * spread * level
    return jnp.minimum(jnp.maximum(result, -limit), limit).astype(kind)


def setup_inputs(seed: int = 0) -> dict:
    keys = jax.random.split(jax.random.key(seed), 14)
    return {
        "coefficient": jnp.clip(jnp.exp(math.log(0.18) - 2.1972246 * jax.random.uniform(keys[0], (NX, NY, NZ), jnp.float32) ** level_of(keys[0], (NX, NY, NZ), ((0, 4),), -0.2, 0.2)), 0.02, 0.18),
        "fwd_older": noise(keys[1], (SHOTS, NX, NY, NZ), 1.0, 6.0, ((0, 8), (1, 4)), jnp.float32),
        "fwd_recent": noise(keys[2], (SHOTS, NX, NY, NZ), 1.0, 6.0, ((0, 8), (1, 4)), jnp.float32),
        "adj_later": noise(keys[3], (SHOTS, NX, NY, NZ), 1.0, 6.0, ((0, 8), (1, 4)), jnp.float32),
        "adj_recent": noise(keys[4], (SHOTS, NX, NY, NZ), 1.0, 6.0, ((0, 8), (1, 4)), jnp.float32),
        "source_xcell": with_ends(jax.random.randint(keys[5], (SHOTS,), 0, NX), jax.random.fold_in(keys[5], 1), 0, NX - 1).astype(jnp.int32),
        "source_ycell": with_ends(jax.random.randint(keys[6], (SHOTS,), 0, NY), jax.random.fold_in(keys[6], 1), 0, NY - 1).astype(jnp.int32),
        "source_zcell": with_ends(jax.random.randint(keys[7], (SHOTS,), 0, NZ), jax.random.fold_in(keys[7], 1), 0, NZ - 1).astype(jnp.int32),
        "amplitude": jnp.clip(1773.62 + 1773.62 * jax.random.uniform(keys[8], (SHOTS, 2), jnp.float32) ** level_of(keys[8], (SHOTS, 2), ((0, 8),), -0.2, 0.2), 1773.62, 3547.24),
        "receiver_xcell": with_ends(jax.random.randint(keys[9], (SHOTS, RECV), 0, NX), jax.random.fold_in(keys[9], 1), 0, NX - 1).astype(jnp.int32),
        "receiver_ycell": with_ends(jax.random.randint(keys[10], (SHOTS, RECV), 0, NY), jax.random.fold_in(keys[10], 1), 0, NY - 1).astype(jnp.int32),
        "receiver_zcell": with_ends(jax.random.randint(keys[11], (SHOTS, RECV), 0, NZ), jax.random.fold_in(keys[11], 1), 0, NZ - 1).astype(jnp.int32),
        "observed": noise(keys[12], (SHOTS, 2, RECV), 1.0, 6.0, ((0, 8),), jnp.float32),
    }


stencil_weights = (-205.0 / 72.0, 8.0 / 5.0, -1.0 / 5.0, 8.0 / 315.0, -1.0 / 560.0)


def laplace_core(extended):
    count = extended.shape[0] - 2 * R
    center = extended[R:R + count]
    width_y = center.shape[1]
    width_z = center.shape[2]
    total = 3.0 * stencil_weights[0] * center
    padded = jnp.pad(center, ((0, 0), (R, R), (R, R)))
    for offset in range(1, R + 1):
        weight = stencil_weights[offset]
        total = total + weight * (extended[R + offset:R + offset + count] + extended[R - offset:R - offset + count])
        total = total + weight * (padded[:, R + offset:R + offset + width_y, R:R + width_z] + padded[:, R - offset:R - offset + width_y, R:R + width_z])
        total = total + weight * (padded[:, R:R + width_y, R + offset:R + offset + width_z] + padded[:, R:R + width_y, R - offset:R - offset + width_z])
    return total


def point_grid(shape, xcells, ycells, zcells, values, start):
    count = shape[0]
    inside = (xcells >= start) & (xcells < start + count)
    local = jnp.clip(xcells - start, 0, count - 1).astype(jnp.int32)
    kept = jnp.where(inside, values, jnp.zeros_like(values))
    return jnp.zeros(shape, values.dtype).at[local, ycells, zcells].add(kept)


def widen(field):
    return jnp.pad(field, ((R, R), (0, 0), (0, 0)))


def reference(coefficient, fwd_older, fwd_recent, adj_later, adj_recent, source_xcell, source_ycell, source_zcell, amplitude, receiver_xcell, receiver_ycell, receiver_zcell, observed):
    shape = coefficient.shape

    def one_shot(carry, inputs):
        older, recent, later, adj_now, sxc, syc, szc, wavelet, rxc, ryc, rzc, recorded = inputs
        first = point_grid(shape, sxc[None], syc[None], szc[None], wavelet[0][None], 0)
        second = point_grid(shape, sxc[None], syc[None], szc[None], wavelet[1][None], 0)
        fwd_two = 2.0 * recent - older + coefficient * (laplace_core(widen(recent)) + first)
        fwd_three = 2.0 * fwd_two - recent + coefficient * (laplace_core(widen(fwd_two)) + second)
        resid_two = fwd_two[rxc, ryc, rzc] - recorded[0]
        resid_three = fwd_three[rxc, ryc, rzc] - recorded[1]
        adj_two = 2.0 * adj_now - later + coefficient * (laplace_core(widen(adj_now)) + point_grid(shape, rxc, ryc, rzc, resid_three, 0))
        adj_one = 2.0 * adj_two - adj_now + coefficient * (laplace_core(widen(adj_two)) + point_grid(shape, rxc, ryc, rzc, resid_two, 0))
        term = adj_one * (fwd_two - 2.0 * recent + older) + adj_two * (fwd_three - 2.0 * fwd_two + recent)
        return carry + term, (fwd_three, adj_one)

    start = jnp.zeros(shape, coefficient.dtype)
    gradient, outputs = lax.scan(one_shot, start, (fwd_older, fwd_recent, adj_later, adj_recent, source_xcell, source_ycell, source_zcell, amplitude, receiver_xcell, receiver_ycell, receiver_zcell, observed))
    return outputs[0], outputs[1], gradient
```

```python
import functools

import jax
import jax.numpy as jnp
import numpy as np
from jax import lax
from jax.experimental import pallas as pl
from jax.experimental.pallas import tpu as pltpu
from jax.sharding import PartitionSpec as P

R = 4
CH = 8
MESH = pl.DeviceIdType.MESH
SCALE = 5040.0
W0 = -3.0 * 14350.0
WK = (8064.0, -1008.0, 128.0, -9.0)
P1, Q3, P2, Q2 = range(4)


def band(size):
    out = np.zeros((size, size), np.float32)
    for k, weight in enumerate(WK, 1):
        out += weight * (np.eye(size, k=k) + np.eye(size, k=-k))
    return out


def kernel(
    dims,
    coef,
    older,
    recent,
    later,
    adj,
    srcs,
    amp,
    rcell,
    obs,
    zz,
    yy,
    out_p3,
    out_q1,
    out_g,
    p2,
    q2,
    cnt,
    o2,
    o3,
    grad,
    land,
    halo,
    hsend,
    hrecv,
    gsend,
    grecv,
):
    ndom, nshot = dims
    nx, ny, nz = coef.shape
    rows = CH * ny
    nch = nx // CH
    bits = nshot.bit_length() - 1
    parts = nch
    while parts > 1 and (nch * rows // parts) // nshot < 8:
        parts //= 2
    prow = nch * rows // parts

    dom = lax.axis_index("dom")
    shot = lax.axis_index("shot")
    has_lo = dom > 0
    has_hi = dom < ndom - 1
    bit = [(shot // (1 << b)) % 2 for b in range(bits)]
    partner = [shot + (1 << b) * (1 - 2 * bit[b]) for b in range(bits)]

    barrier = pltpu.get_barrier_semaphore()
    for b in range(bits):
        pl.semaphore_signal(barrier, inc=1, device_id={"shot": partner[b]}, device_id_type=MESH)

    @pl.when(has_lo)
    def _():
        pl.semaphore_signal(barrier, inc=1, device_id={"dom": dom - 1}, device_id_type=MESH)

    @pl.when(has_hi)
    def _():
        pl.semaphore_signal(barrier, inc=1, device_id={"dom": dom + 1}, device_id_type=MESH)

    pl.semaphore_wait(barrier, bits + has_lo.astype(jnp.int32) + has_hi.astype(jnp.int32))

    def down(f, ref):
        return pltpu.make_async_remote_copy(
            src_ref=ref.at[pl.ds(0, R)],
            dst_ref=halo.at[f, 1],
            send_sem=hsend.at[f, 0],
            recv_sem=hrecv.at[f, 1],
            device_id={"dom": dom - 1},
            device_id_type=MESH,
        )

    def up(f, ref):
        return pltpu.make_async_remote_copy(
            src_ref=ref.at[pl.ds(nx - R, R)],
            dst_ref=halo.at[f, 0],
            send_sem=hsend.at[f, 1],
            recv_sem=hrecv.at[f, 0],
            device_id={"dom": dom + 1},
            device_id_type=MESH,
        )

    def send_lo(f, ref):
        @pl.when(has_lo)
        def _():
            down(f, ref).start()

    def send_hi(f, ref):
        @pl.when(has_hi)
        def _():
            up(f, ref).start()

    def recv_lo(f, ref):
        @pl.when(has_lo)
        def _():
            up(f, ref).wait_recv()

    def recv_hi(f, ref):
        @pl.when(has_hi)
        def _():
            down(f, ref).wait_recv()

    def sent(f, ref):
        @pl.when(has_lo)
        def _():
            down(f, ref).wait_send()

        @pl.when(has_hi)
        def _():
            up(f, ref).wait_send()

    send_lo(P1, recent)
    send_hi(P1, recent)
    send_lo(Q3, adj)
    send_hi(Q3, adj)

    edge = jnp.zeros((R, ny, nz), jnp.float32)

    @pl.when(dom == 0)
    def _():
        for f in range(4):
            halo[f, 0] = edge

    @pl.when(dom == ndom - 1)
    def _():
        for f in range(4):
            halo[f, 1] = edge

    base = dom * nx
    rowid = (rcell[0:1, :] - base) * ny + rcell[1:2, :]
    zid = rcell[2:3, :]
    nrecv = rowid.shape[1]
    pick = (lax.broadcasted_iota(jnp.int32, (nx * ny, nrecv), 0) == rowid).astype(jnp.float32).astype(jnp.bfloat16)
    onz = lax.broadcasted_iota(jnp.int32, (nz, nrecv), 0) == zid
    nt = (((1,), (1,)), ((), ()))

    def spread(values):
        side = jnp.where(onz, values, 0.0).astype(jnp.bfloat16)
        return lax.dot_general(pick, side, nt, preferred_element_type=jnp.float32)

    cnt[...] = spread(1.0)
    for ref, t in ((o3, 1), (o2, 0)):
        value = obs[t : t + 1, :]
        high = value.astype(jnp.bfloat16).astype(jnp.float32)
        ref[...] = spread(high)
        ref[...] += spread(value - high)

    def window(ref, f, c):
        low = ref[c * CH - R : c * CH] if c > 0 else halo[f, 0]
        high = ref[(c + 1) * CH : (c + 1) * CH + R] if c < nch - 1 else halo[f, 1]
        return jnp.concatenate([low, ref[c * CH : (c + 1) * CH], high], axis=0)

    def laplace(ref, f, c):
        ext = window(ref, f, c)
        center = ext[R : R + CH]
        total = W0 * center
        for k, weight in enumerate(WK, 1):
            total = total + weight * (ext[R + k : R + k + CH] + ext[R - k : R - k + CH])
        flat = center.reshape(rows, nz)
        high = flat.astype(jnp.bfloat16)
        low = (flat - high.astype(jnp.float32)).astype(jnp.bfloat16)
        along_z = jnp.dot(jnp.concatenate([high, low], axis=1), zz[...], preferred_element_type=jnp.float32)
        along_y = jnp.dot(yy[...], jnp.concatenate([high, low], axis=0), preferred_element_type=jnp.float32)
        return (total.reshape(rows, nz) + (along_z + along_y)) * (1.0 / SCALE)

    def flat(ref, c):
        return ref[c * CH : (c + 1) * CH].reshape(rows, nz)

    def put(ref, c, value):
        ref[c * CH : (c + 1) * CH] = value.reshape(CH, ny, nz)

    srow = (srcs[0, 0] - base) * ny + srcs[1, 0]
    szed = srcs[2, 0]

    def source(c, t):
        row = lax.broadcasted_iota(jnp.int32, (rows, nz), 0) + c * rows
        lane = lax.broadcasted_iota(jnp.int32, (rows, nz), 1)
        return jnp.where((row == srow) & (lane == szed), amp[0, t], 0.0)

    def at(ref, c):
        return ref[c * rows : (c + 1) * rows, :]

    def step_p2(c):
        value = 2.0 * flat(recent, c) - flat(older, c) + flat(coef, c) * (laplace(recent, P1, c) + source(c, 0))
        put(p2, c, value)

    def step_p3(c):
        value = 2.0 * flat(p2, c) - flat(recent, c) + flat(coef, c) * (laplace(p2, P2, c) + source(c, 1))
        put(out_p3, c, value)

    def step_q2(c):
        points = at(cnt, c) * flat(out_p3, c) - at(o3, c)
        value = 2.0 * flat(adj, c) - flat(later, c) + flat(coef, c) * (laplace(adj, Q3, c) + points)
        put(q2, c, value)

    def step_q1(c):
        two = flat(p2, c)
        points = at(cnt, c) * two - at(o2, c)
        now = flat(q2, c)
        value = 2.0 * now - flat(adj, c) + flat(coef, c) * (laplace(q2, Q2, c) + points)
        put(out_q1, c, value)
        one = flat(recent, c)
        early = two - 2.0 * one + flat(older, c)
        late = flat(out_p3, c) - 2.0 * two + one
        grad[c * rows : (c + 1) * rows, :] = value * early + now * late

    def exchange(p, order):
        off = p * prow
        length = prow
        slot = 0
        pending = []
        for t, b in enumerate(order):
            length //= 2
            keep = pl.multiple_of(off + bit[b] * length, 8)
            give = pl.multiple_of(off + (1 - bit[b]) * length, 8)
            copy = pltpu.make_async_remote_copy(
                src_ref=grad.at[pl.ds(give, length)],
                dst_ref=land.at[pl.ds(p * prow + slot, length)],
                send_sem=gsend.at[p, t],
                recv_sem=grecv.at[p, t],
                device_id={"shot": partner[b]},
                device_id_type=MESH,
            )
            copy.start()
            pending.append(copy)
            yield
            copy.wait_recv()
            total = grad[pl.ds(keep, length), :] + land[p * prow + slot : p * prow + slot + length, :]
            if t < len(order) - 1:
                grad[pl.ds(keep, length), :] = total
            else:
                out_g[pl.ds(keep, length), :] = total
            off = keep
            slot += length
        for t, b in enumerate(reversed(order)):
            copy = pltpu.make_async_remote_copy(
                src_ref=out_g.at[pl.ds(off, length)],
                dst_ref=out_g.at[pl.ds(off, length)],
                send_sem=gsend.at[p, bits + t],
                recv_sem=grecv.at[p, bits + t],
                device_id={"shot": partner[b]},
                device_id_type=MESH,
            )
            copy.start()
            pending.append(copy)
            yield
            copy.wait_recv()
            off = pl.multiple_of(off - bit[b] * length, 8)
            length *= 2
        for copy in pending:
            copy.wait_send()

    edges = (0, nch - 1)
    inner = tuple(range(1, nch - 1))
    per = nch // parts
    ready = set()
    running = []

    def advance():
        for run in list(running):
            if next(run, True):
                running.remove(run)

    def finish(c):
        step_q1(c)
        ready.add(c)
        p = c // per
        if all(i in ready for i in range(p * per, (p + 1) * per)):
            order = list(range(bits))
            if p % 2 and bits > 1:
                order[0], order[1] = order[1], order[0]
            run = exchange(p, order)
            next(run, None)
            running.append(run)

    for c in inner:
        step_p2(c)
    recv_lo(P1, recent)
    step_p2(0)
    send_lo(P2, p2)
    recv_hi(P1, recent)
    step_p2(nch - 1)
    send_hi(P2, p2)
    for c in inner:
        step_p3(c)
        step_q2(c)
    recv_lo(Q3, adj)
    recv_lo(P2, p2)
    step_p3(0)
    step_q2(0)
    send_lo(Q2, q2)
    recv_hi(Q3, adj)
    recv_hi(P2, p2)
    step_p3(nch - 1)
    step_q2(nch - 1)
    send_hi(Q2, q2)
    for c in inner:
        finish(c)
    recv_lo(Q2, q2)
    finish(0)
    recv_hi(Q2, q2)
    finish(nch - 1)
    while running:
        advance()
    sent(P1, recent)
    sent(Q3, adj)
    sent(P2, p2)
    sent(Q2, q2)


def shards(
    coefficient,
    fwd_older,
    fwd_recent,
    adj_later,
    adj_recent,
    source_xcell,
    source_ycell,
    source_zcell,
    amplitude,
    receiver_xcell,
    receiver_ycell,
    receiver_zcell,
    observed,
):
    ndom, nshot = lax.axis_size("dom"), lax.axis_size("shot")
    nx, ny, nz = coefficient.shape
    cells = nx * ny
    bits = nshot.bit_length() - 1
    zmat = band(nz)
    ymat = np.kron(np.eye(CH), band(ny))
    zz = jnp.asarray(np.concatenate([zmat, zmat], 0), jnp.bfloat16)
    yy = jnp.asarray(np.concatenate([ymat, ymat], 1), jnp.bfloat16)
    srcs = jnp.stack([source_xcell, source_ycell, source_zcell])
    rcell = jnp.concatenate([receiver_xcell, receiver_ycell, receiver_zcell])
    field = jax.ShapeDtypeStruct((nx, ny, nz), jnp.float32)
    vmem = pl.BlockSpec(memory_space=pltpu.VMEM)
    smem = pl.BlockSpec(memory_space=pltpu.SMEM)
    block = pltpu.VMEM((nx, ny, nz), jnp.float32)
    plane = pltpu.VMEM((cells, nz), jnp.float32)
    p3, q1, grad = pl.pallas_call(
        functools.partial(kernel, (ndom, nshot)),
        out_shape=(field, field, jax.ShapeDtypeStruct((cells, nz), jnp.float32)),
        in_specs=[vmem] * 5 + [smem] * 2 + [vmem] * 4,
        out_specs=(vmem,) * 3,
        scratch_shapes=[
            block,
            block,
            plane,
            plane,
            plane,
            plane,
            plane,
            pltpu.VMEM((4, 2, R, ny, nz), jnp.float32),
            pltpu.SemaphoreType.DMA((4, 2)),
            pltpu.SemaphoreType.DMA((4, 2)),
            pltpu.SemaphoreType.DMA((nx // CH, 2 * bits)),
            pltpu.SemaphoreType.DMA((nx // CH, 2 * bits)),
        ],
        compiler_params=pltpu.CompilerParams(
            collective_id=0, has_side_effects=True, vmem_limit_bytes=48 * 1024 * 1024
        ),
        cost_estimate=pl.CostEstimate(flops=4 * 10**9, bytes_accessed=8 * 4 * cells * nz, transcendentals=0),
        name="wave_steps",
    )(
        coefficient,
        fwd_older[0],
        fwd_recent[0],
        adj_later[0],
        adj_recent[0],
        srcs,
        amplitude,
        rcell,
        observed[0],
        zz,
        yy,
    )
    return p3[None], q1[None], grad.reshape(nx, ny, nz)


def solution(mesh):
    return jax.shard_map(
        shards,
        mesh=mesh,
        in_specs=(
            P("dom", None, None),
            P("shot", "dom", None, None),
            P("shot", "dom", None, None),
            P("shot", "dom", None, None),
            P("shot", "dom", None, None),
            P("shot"),
            P("shot"),
            P("shot"),
            P("shot", None),
            P("shot", None),
            P("shot", None),
            P("shot", None),
            P("shot", None, None),
        ),
        out_specs=(
            P("shot", "dom", None, None),
            P("shot", "dom", None, None),
            P("dom", None, None),
        ),
        check_vma=False,
    )
```

```python
import functools

import jax
import jax.numpy as jnp
from jax import lax
from jax.experimental import pallas as pl
from jax.experimental.pallas import tpu as pltpu
from jax.sharding import PartitionSpec as P

R = 4
CH = 8
MESH = pl.DeviceIdType.MESH
SCALE = 5040.0
W0 = -3.0 * 14350.0
WK = (8064.0, -1008.0, 128.0, -9.0)
P1, Q3, P2, Q2 = range(4)


def band(size, group):
    row = lax.broadcasted_iota(jnp.int32, (size, size), 0)
    col = lax.broadcasted_iota(jnp.int32, (size, size), 1)
    apart = jnp.abs(row - col)
    out = jnp.zeros((size, size), jnp.float32)
    for k, weight in enumerate(WK, 1):
        out = jnp.where(apart == k, weight, out)
    if group < size:
        out = jnp.where(row // group == col // group, out, 0.0)
    return out.astype(jnp.bfloat16)


def kernel(
    dims,
    coef_in,
    older_in,
    recent_in,
    later_in,
    adj_in,
    sx,
    sy,
    sz,
    amp,
    rx,
    ry,
    rz,
    obs,
    out_p3,
    out_q1,
    out_g,
    p3,
    q1,
    gsum,
    coef,
    older,
    later,
    p1,
    q3,
    p2,
    q2,
    zz,
    yy,
    cnt,
    o2,
    o3,
    grad,
    land,
    load,
    save,
    hsend,
    hrecv,
    gsend,
    grecv,
):
    ndom, nshot = dims
    nx, ny, nz = coef.shape
    rows = CH * ny
    nch = nx // CH
    bits = nshot.bit_length() - 1
    parts = gsend.shape[0]
    prow = nx * ny // parts

    dom = lax.axis_index("dom")
    shot = lax.axis_index("shot")
    has_lo = dom > 0
    has_hi = dom < ndom - 1
    bit = [(shot // (1 << b)) % 2 for b in range(bits)]
    partner = [shot + (1 << b) * (1 - 2 * bit[b]) for b in range(bits)]

    own = pl.ds(R, nx)
    loads = [
        pltpu.make_async_copy(src, dst, load.at[i])
        for i, (src, dst) in enumerate(
            (
                (recent_in, p1.at[own]),
                (older_in, older),
                (coef_in, coef),
                (adj_in, q3.at[own]),
                (later_in, later),
            )
        )
    ]
    for copy in loads:
        copy.start()

    barrier = pltpu.get_barrier_semaphore()
    for b in range(bits):
        pl.semaphore_signal(barrier, inc=1, device_id={"shot": partner[b]}, device_id_type=MESH)

    @pl.when(has_lo)
    def _():
        pl.semaphore_signal(barrier, inc=1, device_id={"dom": dom - 1}, device_id_type=MESH)

    @pl.when(has_hi)
    def _():
        pl.semaphore_signal(barrier, inc=1, device_id={"dom": dom + 1}, device_id_type=MESH)

    pl.semaphore_wait(barrier, bits + has_lo.astype(jnp.int32) + has_hi.astype(jnp.int32))

    def down(f, src, first, ref):
        return pltpu.make_async_remote_copy(
            src_ref=src.at[pl.ds(first, R)],
            dst_ref=ref.at[pl.ds(R + nx, R)],
            send_sem=hsend.at[f, 0],
            recv_sem=hrecv.at[f, 1],
            device_id={"dom": dom - 1},
            device_id_type=MESH,
        )

    def up(f, src, first, ref):
        return pltpu.make_async_remote_copy(
            src_ref=src.at[pl.ds(first + nx - R, R)],
            dst_ref=ref.at[pl.ds(0, R)],
            send_sem=hsend.at[f, 1],
            recv_sem=hrecv.at[f, 0],
            device_id={"dom": dom + 1},
            device_id_type=MESH,
        )

    def both(act, f, src, first, ref):
        @pl.when(has_lo)
        def _():
            act(down, up, f, src, first, ref)

        @pl.when(has_hi)
        def _():
            act(up, down, f, src, first, ref)

    def send(*args):
        both(lambda mine, other, *rest: mine(*rest).start(), *args)

    def receive(*args):
        both(lambda mine, other, *rest: other(*rest).wait_recv(), *args)

    def sent(*args):
        both(lambda mine, other, *rest: mine(*rest).wait_send(), *args)

    halo_p1 = (P1, recent_in, 0, p1)
    halo_q3 = (Q3, adj_in, 0, q3)
    halo_p2 = (P2, p2, R, p2)
    halo_q2 = (Q2, q2, R, q2)
    send(*halo_p1)
    send(*halo_q3)

    zmat = band(nz, nz)
    zz[0:nz, :] = zmat
    zz[nz : 2 * nz, :] = zmat
    ymat = band(rows, ny)
    yy[:, 0:rows] = ymat
    yy[:, rows : 2 * rows] = ymat

    nothing = jnp.zeros((R, ny, nz), jnp.float32)

    @pl.when(dom == 0)
    def _():
        for ref in (p1, q3, p2, q2):
            ref[0:R] = nothing

    @pl.when(dom == ndom - 1)
    def _():
        for ref in (p1, q3, p2, q2):
            ref[R + nx : R + nx + R] = nothing

    base = dom * nx
    nrecv = rx.shape[1]
    rowid = (rx[...] - base) * ny + ry[...]
    pick = (lax.broadcasted_iota(jnp.int32, (nx * ny, nrecv), 0) == rowid).astype(jnp.float32).astype(jnp.bfloat16)
    onz = lax.broadcasted_iota(jnp.int32, (nz, nrecv), 0) == rz[...]
    nt = (((1,), (1,)), ((), ()))

    def spread(values):
        side = jnp.where(onz, values, 0.0).astype(jnp.bfloat16)
        return lax.dot_general(pick, side, nt, preferred_element_type=jnp.float32)

    def observe(t):
        value = obs[t : t + 1, :]
        high = value.astype(jnp.bfloat16).astype(jnp.float32)
        return spread(high) + spread(value - high)

    def laplace(ref, c):
        ext = ref[pl.ds(c * CH, CH + 2 * R)]
        center = ext[R : R + CH]
        total = W0 * center
        for k, weight in enumerate(WK, 1):
            total = total + weight * (ext[R + k : R + k + CH] + ext[R - k : R - k + CH])
        flat = center.reshape(rows, nz)
        high = flat.astype(jnp.bfloat16)
        low = (flat - high.astype(jnp.float32)).astype(jnp.bfloat16)
        along_z = jnp.dot(jnp.concatenate([high, low], axis=1), zz[...], preferred_element_type=jnp.float32)
        along_y = jnp.dot(yy[...], jnp.concatenate([high, low], axis=0), preferred_element_type=jnp.float32)
        return (total.reshape(rows, nz) + (along_z + along_y)) * (1.0 / SCALE)

    def flat(ref, c, first=0):
        return ref[pl.ds(first + c * CH, CH)].reshape(rows, nz)

    def put(ref, c, value, first=0):
        ref[pl.ds(first + c * CH, CH)] = value.reshape(CH, ny, nz)

    def at(c):
        return pl.ds(pl.multiple_of(c * rows, rows), rows)

    srow = (sx[0] - base) * ny + sy[0]
    szed = sz[0]

    def source(c, t):
        row = lax.broadcasted_iota(jnp.int32, (rows, 1), 0) + c * rows
        lane = lax.broadcasted_iota(jnp.int32, (1, nz), 1)
        return jnp.where(row == srow, amp[0, t], 0.0) * jnp.where(lane == szed, 1.0, 0.0)

    def step_p2(c):
        value = 2.0 * flat(p1, c, R) - flat(older, c) + flat(coef, c) * (laplace(p1, c) + source(c, 0))
        put(p2, c, value, R)

    def step_p3(c):
        value = 2.0 * flat(p2, c, R) - flat(p1, c, R) + flat(coef, c) * (laplace(p2, c) + source(c, 1))
        put(p3, c, value)

    def step_q2(c):
        points = cnt[at(c), :] * flat(p3, c) - o3[at(c), :]
        value = 2.0 * flat(q3, c, R) - flat(later, c) + flat(coef, c) * (laplace(q3, c) + points)
        put(q2, c, value, R)

    def step_q1(c):
        two = flat(p2, c, R)
        points = cnt[at(c), :] * two - o2[at(c), :]
        now = flat(q2, c, R)
        value = 2.0 * now - flat(q3, c, R) + flat(coef, c) * (laplace(q2, c) + points)
        put(q1, c, value)
        one = flat(p1, c, R)
        early = two - 2.0 * one + flat(older, c)
        late = flat(p3, c) - 2.0 * two + one
        grad[at(c), :] = value * early + now * late

    def sweep(before_edges, body):
        def turn(i, carry):
            @pl.when(i == nch - 2)
            def _():
                before_edges()

            body(lax.rem(i + 1, nch))
            return carry

        lax.fori_loop(0, nch, turn, 0)

    def order_of(h):
        order = list(range(bits))
        if h and bits > 1:
            order[0], order[1] = order[1], order[0]
        return order

    def place(p, h, t):
        off = p * prow
        for u, b in enumerate(order_of(h)[:t]):
            off = off + bit[b] * (prow >> (u + 1))
        return off

    def rows_at(off, length):
        return pl.ds(pl.multiple_of(off, 8), length)

    def slot(p, t):
        return rows_at(p * prow + prow - (prow >> t), prow >> (t + 1))

    def reduce_copy(p, h, t):
        b = order_of(h)[t]
        length = prow >> (t + 1)
        give = place(p, h, t) + (1 - bit[b]) * length
        return pltpu.make_async_remote_copy(
            src_ref=grad.at[rows_at(give, length)],
            dst_ref=land.at[slot(p, t)],
            send_sem=gsend.at[p, t],
            recv_sem=grecv.at[p, t],
            device_id={"shot": partner[b]},
            device_id_type=MESH,
        )

    def gather_copy(p, h, t):
        rows_held = rows_at(place(p, h, t + 1), prow >> (t + 1))
        return pltpu.make_async_remote_copy(
            src_ref=gsum.at[rows_held],
            dst_ref=gsum.at[rows_held],
            send_sem=gsend.at[p, bits + t],
            recv_sem=grecv.at[p, bits + t],
            device_id={"shot": partner[order_of(h)[t]]},
            device_id_type=MESH,
        )

    def save_sum(p):
        return pltpu.make_async_copy(gsum.at[rows_at(p * prow, prow)], out_g.at[rows_at(p * prow, prow)], save.at[2 + p])

    def advance(p, h, n):
        if n < bits:
            reduce_copy(p, h, n).wait_recv()
            keep = rows_at(place(p, h, n + 1), prow >> (n + 1))
            total = grad[keep, :] + land[slot(p, n), :]
            if n < bits - 1:
                grad[keep, :] = total
                reduce_copy(p, h, n + 1).start()
            else:
                gsum[keep, :] = total
                gather_copy(p, h, bits - 1).start()
        else:
            t = 2 * bits - 1 - n
            gather_copy(p, h, t).wait_recv()
            if t:
                gather_copy(p, h, t - 1).start()
            else:
                save_sum(p).start()

    cnt[...] = spread(1.0)
    o3[...] = observe(1)
    for copy in loads[:3]:
        copy.wait()
    sweep(lambda: receive(*halo_p1), step_p2)
    send(*halo_p2)
    o2[...] = observe(0)
    for copy in loads[3:]:
        copy.wait()

    def middle(c):
        step_p3(c)
        step_q2(c)

    def arrive():
        receive(*halo_q3)
        receive(*halo_p2)

    sweep(arrive, middle)
    send(*halo_q2)
    save_p3 = pltpu.make_async_copy(p3, out_p3, save.at[0])
    save_q1 = pltpu.make_async_copy(q1, out_q1, save.at[1])
    save_p3.start()
    per = max(parts // nch, 1)

    def last(c):
        step_q1(c)
        if parts >= nch:
            for h in range(per):
                reduce_copy(c * per + h, h % 2, 0).start()

    sweep(lambda: receive(*halo_q2), last)
    save_q1.start()
    if parts < nch:
        for p in range(parts):
            reduce_copy(p, p % 2, 0).start()
    groups = [[(((c + 1) % nch) * per + h, h % 2) for h in range(per)] for c in range(nch)]
    if parts < nch:
        groups = [[(p, p % 2)] for p in range(parts)]
    steps = 2 * bits
    for turn in range(steps + len(groups) - 1):
        for g, group in enumerate(groups):
            if 0 <= turn - g < steps:
                for p, h in group:
                    advance(p, h, turn - g)
    for p in range(parts):
        h = (p % per) % 2 if parts >= nch else p % 2
        for t in range(bits):
            reduce_copy(p, h, t).wait_send()
            gather_copy(p, h, t).wait_send()
        save_sum(p).wait()
    save_p3.wait()
    save_q1.wait()
    sent(*halo_p1)
    sent(*halo_q3)
    sent(*halo_p2)
    sent(*halo_q2)


def store_kernel(a, b, c, out_a, out_b, out_c, sem):
    copies = [
        pltpu.make_async_copy(src, dst, sem.at[i])
        for i, (src, dst) in enumerate(((a, out_a), (b, out_b), (c, out_c)))
    ]
    for copy in copies:
        copy.start()
    for copy in copies:
        copy.wait()


def shards(
    coefficient,
    fwd_older,
    fwd_recent,
    adj_later,
    adj_recent,
    source_xcell,
    source_ycell,
    source_zcell,
    amplitude,
    receiver_xcell,
    receiver_ycell,
    receiver_zcell,
    observed,
):
    ndom, nshot = lax.axis_size("dom"), lax.axis_size("shot")
    nx, ny, nz = coefficient.shape
    cells = nx * ny
    bits = nshot.bit_length() - 1
    rows = CH * ny
    field = jax.ShapeDtypeStruct((nx, ny, nz), jnp.float32)
    plane_out = jax.ShapeDtypeStruct((cells, nz), jnp.float32)
    parts = 2 * (nx // CH)
    while parts > 1 and (cells // parts) // nshot < 8:
        parts //= 2
    hbm = pl.BlockSpec(memory_space=pltpu.HBM)
    vmem = pl.BlockSpec(memory_space=pltpu.VMEM)
    smem = pl.BlockSpec(memory_space=pltpu.SMEM)
    block = pltpu.VMEM((nx, ny, nz), jnp.float32)
    wide = pltpu.VMEM((nx + 2 * R, ny, nz), jnp.float32)
    plane = pltpu.VMEM((cells, nz), jnp.float32)
    p3, q1, grad = pl.pallas_call(
        functools.partial(kernel, (ndom, nshot)),
        out_shape=(field, field, plane_out),
        in_specs=[hbm] * 5 + [smem] * 4 + [vmem] * 4,
        out_specs=(hbm,) * 3,
        scratch_shapes=[block] * 2
        + [plane]
        + [block] * 3
        + [wide] * 4
        + [pltpu.VMEM((2 * nz, nz), jnp.bfloat16), pltpu.VMEM((rows, 2 * rows), jnp.bfloat16)]
        + [plane] * 5
        + [
            pltpu.SemaphoreType.DMA((5,)),
            pltpu.SemaphoreType.DMA((2 + parts,)),
            pltpu.SemaphoreType.DMA((4, 2)),
            pltpu.SemaphoreType.DMA((4, 2)),
            pltpu.SemaphoreType.DMA((parts, 2 * bits)),
            pltpu.SemaphoreType.DMA((parts, 2 * bits)),
        ],
        compiler_params=pltpu.CompilerParams(
            collective_id=0, has_side_effects=True, vmem_limit_bytes=60 * 1024 * 1024
        ),
        cost_estimate=pl.CostEstimate(flops=4 * 10**9, bytes_accessed=8 * 4 * cells * nz, transcendentals=0),
        name="wave_steps",
    )(
        coefficient,
        fwd_older[0],
        fwd_recent[0],
        adj_later[0],
        adj_recent[0],
        source_xcell,
        source_ycell,
        source_zcell,
        amplitude,
        receiver_xcell,
        receiver_ycell,
        receiver_zcell,
        observed[0],
    )
    p3, q1, grad = pl.pallas_call(
        store_kernel,
        out_shape=(field, field, plane_out),
        in_specs=[hbm] * 3,
        out_specs=(hbm,) * 3,
        scratch_shapes=[pltpu.SemaphoreType.DMA((3,))],
        compiler_params=pltpu.CompilerParams(vmem_limit_bytes=60 * 1024 * 1024),
        cost_estimate=pl.CostEstimate(flops=0, bytes_accessed=6 * 4 * cells * nz, transcendentals=0),
        name="store_results",
    )(p3, q1, grad)
    return p3[None], q1[None], grad.reshape(nx, ny, nz)


def solution(mesh):
    return jax.shard_map(
        shards,
        mesh=mesh,
        in_specs=(
            P("dom", None, None),
            P("shot", "dom", None, None),
            P("shot", "dom", None, None),
            P("shot", "dom", None, None),
            P("shot", "dom", None, None),
            P("shot"),
            P("shot"),
            P("shot"),
            P("shot", None),
            P("shot", None),
            P("shot", None),
            P("shot", None),
            P("shot", None, None),
        ),
        out_specs=(
            P("shot", "dom", None, None),
            P("shot", "dom", None, None),
            P("dom", None, None),
        ),
        check_vma=False,
    )
```

```python
import functools

import jax
import jax.numpy as jnp
from jax import lax
from jax.experimental import pallas as pl
from jax.experimental.pallas import tpu as pltpu
from jax.sharding import PartitionSpec as P

R = 4
CH = 8
MESH = pl.DeviceIdType.MESH
SCALE = 5040.0
W0 = -3.0 * 14350.0
WK = (8064.0, -1008.0, 128.0, -9.0)
P1, Q3, P2, Q2 = range(4)


def band(size, group):
    row = lax.broadcasted_iota(jnp.int32, (size, size), 0)
    col = lax.broadcasted_iota(jnp.int32, (size, size), 1)
    apart = jnp.abs(row - col)
    out = jnp.zeros((size, size), jnp.float32)
    for k, weight in enumerate(WK, 1):
        out = jnp.where(apart == k, weight, out)
    if group < size:
        out = jnp.where(row // group == col // group, out, 0.0)
    return out.astype(jnp.bfloat16)


def kernel(
    dims,
    coef_in,
    older_in,
    recent_in,
    later_in,
    adj_in,
    sx,
    sy,
    sz,
    amp,
    rx,
    ry,
    rz,
    obs,
    out_p3,
    out_q1,
    out_g,
    p3,
    q1,
    gsum,
    coef,
    older,
    later,
    p1,
    q3,
    p2,
    q2,
    zz,
    yy,
    cnt,
    o2,
    o3,
    grad,
    land,
    load,
    save,
    hsend,
    hrecv,
    gsend,
    grecv,
):
    ndom, nshot = dims
    nx, ny, nz = coef.shape
    rows = CH * ny
    npair = nx // CH
    slab = R * ny
    bits = nshot.bit_length() - 1
    parts = gsend.shape[0]
    prow = nx * ny // parts

    dom = lax.axis_index("dom")
    shot = lax.axis_index("shot")
    has_lo = dom > 0
    has_hi = dom < ndom - 1
    bit = [(shot // (1 << b)) % 2 for b in range(bits)]
    partner = [shot + (1 << b) * (1 - 2 * bit[b]) for b in range(bits)]

    own = pl.ds(R, nx)
    loads = [
        pltpu.make_async_copy(src, dst, load.at[i])
        for i, (src, dst) in enumerate(
            (
                (recent_in, p1.at[own]),
                (older_in, older),
                (coef_in, coef),
                (adj_in, q3.at[own]),
                (later_in, later),
            )
        )
    ]
    for copy in loads:
        copy.start()

    barrier = pltpu.get_barrier_semaphore()
    for b in range(bits):
        pl.semaphore_signal(barrier, inc=1, device_id={"shot": partner[b]}, device_id_type=MESH)

    @pl.when(has_lo)
    def _():
        pl.semaphore_signal(barrier, inc=1, device_id={"dom": dom - 1}, device_id_type=MESH)

    @pl.when(has_hi)
    def _():
        pl.semaphore_signal(barrier, inc=1, device_id={"dom": dom + 1}, device_id_type=MESH)

    pl.semaphore_wait(barrier, bits + has_lo.astype(jnp.int32) + has_hi.astype(jnp.int32))

    def down(f, src, first, ref):
        return pltpu.make_async_remote_copy(
            src_ref=src.at[pl.ds(first, R)],
            dst_ref=ref.at[pl.ds(R + nx, R)],
            send_sem=hsend.at[f, 0],
            recv_sem=hrecv.at[f, 1],
            device_id={"dom": dom - 1},
            device_id_type=MESH,
        )

    def up(f, src, first, ref):
        return pltpu.make_async_remote_copy(
            src_ref=src.at[pl.ds(first + nx - R, R)],
            dst_ref=ref.at[pl.ds(0, R)],
            send_sem=hsend.at[f, 1],
            recv_sem=hrecv.at[f, 0],
            device_id={"dom": dom + 1},
            device_id_type=MESH,
        )

    def both(act, f, src, first, ref):
        @pl.when(has_lo)
        def _():
            act(down, up, f, src, first, ref)

        @pl.when(has_hi)
        def _():
            act(up, down, f, src, first, ref)

    def send(*args):
        both(lambda mine, other, *rest: mine(*rest).start(), *args)

    def receive(*args):
        both(lambda mine, other, *rest: other(*rest).wait_recv(), *args)

    def sent(*args):
        both(lambda mine, other, *rest: mine(*rest).wait_send(), *args)

    halo_p1 = (P1, recent_in, 0, p1)
    halo_q3 = (Q3, adj_in, 0, q3)
    halo_p2 = (P2, p2, R, p2)
    halo_q2 = (Q2, q2, R, q2)
    send(*halo_p1)
    send(*halo_q3)

    zmat = band(nz, nz)
    zz[0:nz, :] = zmat
    zz[nz : 2 * nz, :] = zmat
    ymat = band(rows, ny)
    yy[:, 0:rows] = ymat
    yy[:, rows : 2 * rows] = ymat

    nothing = jnp.zeros((R, ny, nz), jnp.float32)

    @pl.when(dom == 0)
    def _():
        for ref in (p1, q3, p2, q2):
            ref[0:R] = nothing

    @pl.when(dom == ndom - 1)
    def _():
        for ref in (p1, q3, p2, q2):
            ref[R + nx : R + nx + R] = nothing

    base = dom * nx
    nrecv = rx.shape[1]
    rowid = (rx[...] - base) * ny + ry[...]
    pick = (lax.broadcasted_iota(jnp.int32, (nx * ny, nrecv), 0) == rowid).astype(jnp.float32).astype(jnp.bfloat16)
    onz = lax.broadcasted_iota(jnp.int32, (nz, nrecv), 0) == rz[...]
    nt = (((1,), (1,)), ((), ()))

    def spread(values):
        side = jnp.where(onz, values, 0.0).astype(jnp.bfloat16)
        return lax.dot_general(pick, side, nt, preferred_element_type=jnp.float32)

    def observe(t):
        value = obs[t : t + 1, :]
        high = value.astype(jnp.bfloat16).astype(jnp.float32)
        return spread(high) + spread(value - high)

    def slabs(c):
        return c * R, nx - R - c * R

    def laplace(ref, c):
        sides = [ref[pl.ds(first, 3 * R)] for first in slabs(c)]

        def shifted(k):
            return jnp.concatenate([side[R + k : 2 * R + k] for side in sides], axis=0)

        center = shifted(0)
        total = W0 * center
        for k, weight in enumerate(WK, 1):
            total = total + weight * (shifted(k) + shifted(-k))
        flat = center.reshape(rows, nz)
        high = flat.astype(jnp.bfloat16)
        low = (flat - high.astype(jnp.float32)).astype(jnp.bfloat16)
        along_z = jnp.dot(jnp.concatenate([high, low], axis=1), zz[...], preferred_element_type=jnp.float32)
        along_y = jnp.dot(yy[...], jnp.concatenate([high, low], axis=0), preferred_element_type=jnp.float32)
        return (total.reshape(rows, nz) + (along_z + along_y)) * (1.0 / SCALE)

    def flat(ref, c, skip=0):
        return jnp.concatenate([ref[pl.ds(skip + first, R)] for first in slabs(c)], axis=0).reshape(rows, nz)

    def put(ref, c, value, skip=0):
        value = value.reshape(CH, ny, nz)
        for i, first in enumerate(slabs(c)):
            ref[pl.ds(skip + first, R)] = value[i * R : (i + 1) * R]

    def slab_rows(first):
        return pl.ds(pl.multiple_of(first * ny, slab), slab)

    def take(ref, c):
        return jnp.concatenate([ref[slab_rows(first), :] for first in slabs(c)], axis=0)

    srow = (sx[0] - base) * ny + sy[0]
    szed = sz[0]

    def source(c, t):
        row = lax.broadcasted_iota(jnp.int32, (rows, 1), 0)
        row = row + jnp.where(row < slab, c * slab, (nx - CH - c * R) * ny)
        lane = lax.broadcasted_iota(jnp.int32, (1, nz), 1)
        return jnp.where(row == srow, amp[0, t], 0.0) * jnp.where(lane == szed, 1.0, 0.0)

    def step_p2(c):
        value = 2.0 * flat(p1, c, R) - flat(older, c) + flat(coef, c) * (laplace(p1, c) + source(c, 0))
        put(p2, c, value, R)

    def step_p3(c):
        value = 2.0 * flat(p2, c, R) - flat(p1, c, R) + flat(coef, c) * (laplace(p2, c) + source(c, 1))
        put(p3, c, value)

    def step_q2(c):
        points = take(cnt, c) * flat(p3, c) - take(o3, c)
        value = 2.0 * flat(q3, c, R) - flat(later, c) + flat(coef, c) * (laplace(q3, c) + points)
        put(q2, c, value, R)

    def step_q1(c):
        two = flat(p2, c, R)
        points = take(cnt, c) * two - take(o2, c)
        now = flat(q2, c, R)
        value = 2.0 * now - flat(q3, c, R) + flat(coef, c) * (laplace(q2, c) + points)
        put(q1, c, value)
        one = flat(p1, c, R)
        early = two - 2.0 * one + flat(older, c)
        late = flat(p3, c) - 2.0 * two + one
        term = value * early + now * late
        for i, first in enumerate(slabs(c)):
            grad[slab_rows(first), :] = term[i * slab : (i + 1) * slab]

    def order_of(h):
        order = list(range(bits))
        if h and bits > 1:
            order[0], order[1] = order[1], order[0]
        return order

    def place(p, h, t):
        off = p * prow
        for u, b in enumerate(order_of(h)[:t]):
            off = off + bit[b] * (prow >> (u + 1))
        return off

    def rows_at(off, length):
        return pl.ds(pl.multiple_of(off, 8), length)

    def slot(p, t):
        return rows_at(p * prow + prow - (prow >> t), prow >> (t + 1))

    def reduce_copy(p, h, t):
        b = order_of(h)[t]
        length = prow >> (t + 1)
        give = place(p, h, t) + (1 - bit[b]) * length
        return pltpu.make_async_remote_copy(
            src_ref=grad.at[rows_at(give, length)],
            dst_ref=land.at[slot(p, t)],
            send_sem=gsend.at[p, t],
            recv_sem=grecv.at[p, t],
            device_id={"shot": partner[b]},
            device_id_type=MESH,
        )

    def gather_copy(p, h, t):
        rows_held = rows_at(place(p, h, t + 1), prow >> (t + 1))
        return pltpu.make_async_remote_copy(
            src_ref=gsum.at[rows_held],
            dst_ref=gsum.at[rows_held],
            send_sem=gsend.at[p, bits + t],
            recv_sem=grecv.at[p, bits + t],
            device_id={"shot": partner[order_of(h)[t]]},
            device_id_type=MESH,
        )

    def save_sum(p):
        return pltpu.make_async_copy(gsum.at[rows_at(p * prow, prow)], out_g.at[rows_at(p * prow, prow)], save.at[2 + p])

    def advance(p, h, n):
        if n < bits:
            reduce_copy(p, h, n).wait_recv()
            keep = rows_at(place(p, h, n + 1), prow >> (n + 1))
            total = grad[keep, :] + land[slot(p, n), :]
            if n < bits - 1:
                grad[keep, :] = total
                reduce_copy(p, h, n + 1).start()
            else:
                gsum[keep, :] = total
                gather_copy(p, h, bits - 1).start()
        else:
            t = 2 * bits - 1 - n
            gather_copy(p, h, t).wait_recv()
            if t:
                gather_copy(p, h, t - 1).start()
            else:
                save_sum(p).start()

    early_start = parts == 2 * npair

    def group(c):
        return ((c, 0), (parts - 1 - c, c % 2)) if early_start else ((c, c % 2),)

    cnt[...] = spread(1.0)
    o3[...] = observe(1)
    for copy in loads[:3]:
        copy.wait()

    def first_turn(i, carry):
        @pl.when(i == npair - 1)
        def _():
            receive(*halo_p1)

        step_p2(npair - 1 - i)
        return carry

    lax.fori_loop(0, npair, first_turn, 0)
    send(*halo_p2)
    o2[...] = observe(0)
    for copy in loads[3:]:
        copy.wait()

    save_p3 = pltpu.make_async_copy(p3, out_p3, save.at[0])
    save_q1 = pltpu.make_async_copy(q1, out_q1, save.at[1])

    def turn(i, carry):
        @pl.when(i == npair - 1)
        def _():
            receive(*halo_q3)
            receive(*halo_p2)

        @pl.when(i < npair)
        def _():
            step_p3(npair - 1 - i)
            step_q2(npair - 1 - i)

        @pl.when(i == npair - 1)
        def _():
            send(*halo_q2)
            save_p3.start()

        @pl.when(i == npair)
        def _():
            receive(*halo_q2)

        @pl.when(i > 0)
        def _():
            step_q1(npair - i)

        if early_start:
            for c in range(npair):

                @pl.when(i == npair - c)
                def _():
                    for p, h in group(c):
                        reduce_copy(p, h, 0).start()

                for n in range(c):

                    @pl.when(i == npair - c + 1 + n)
                    def _():
                        for p, h in group(c):
                            advance(p, h, n)

        return carry

    lax.fori_loop(0, npair + 1, turn, 0)
    save_q1.start()
    steps = 2 * bits
    if early_start:
        left = [(c, c) for c in reversed(range(npair))]
    else:
        left = [(p, 0) for p in range(parts)]
        for p, _ in left:
            for portion in group(p):
                reduce_copy(*portion, 0).start()
    while left:
        for c, n in left:
            for p, h in group(c):
                advance(p, h, n)
        left = [(c, n + 1) for c, n in left if n + 1 < steps]
    for c in range(npair if early_start else parts):
        for p, h in group(c):
            for t in range(bits):
                reduce_copy(p, h, t).wait_send()
                gather_copy(p, h, t).wait_send()
            save_sum(p).wait()
    save_p3.wait()
    save_q1.wait()
    sent(*halo_p1)
    sent(*halo_q3)
    sent(*halo_p2)
    sent(*halo_q2)


def store_kernel(a, b, c, out_a, out_b, out_c, va, vb, vc, sem):
    pieces = 2
    moves = []
    for i in range(pieces):
        for k, (src, mid, dst) in enumerate(((a, va, out_a), (b, vb, out_b), (c, vc, out_c))):
            size = src.shape[0] // pieces
            part = pl.ds(i * size, size)
            come = pltpu.make_async_copy(src.at[part], mid.at[part], sem.at[0, i, k])
            go = pltpu.make_async_copy(mid.at[part], dst.at[part], sem.at[1, i, k])
            come.start()
            moves.append((come, go))
    for come, go in moves:
        come.wait()
        go.start()
    for come, go in moves:
        go.wait()


def shards(
    coefficient,
    fwd_older,
    fwd_recent,
    adj_later,
    adj_recent,
    source_xcell,
    source_ycell,
    source_zcell,
    amplitude,
    receiver_xcell,
    receiver_ycell,
    receiver_zcell,
    observed,
):
    ndom, nshot = lax.axis_size("dom"), lax.axis_size("shot")
    nx, ny, nz = coefficient.shape
    cells = nx * ny
    bits = nshot.bit_length() - 1
    rows = CH * ny
    field = jax.ShapeDtypeStruct((nx, ny, nz), jnp.float32)
    plane_out = jax.ShapeDtypeStruct((cells, nz), jnp.float32)
    parts = 2 * (nx // CH)
    while parts > 1 and (cells // parts) // nshot < 8:
        parts //= 2
    hbm = pl.BlockSpec(memory_space=pltpu.HBM)
    vmem = pl.BlockSpec(memory_space=pltpu.VMEM)
    smem = pl.BlockSpec(memory_space=pltpu.SMEM)
    block = pltpu.VMEM((nx, ny, nz), jnp.float32)
    wide = pltpu.VMEM((nx + 2 * R, ny, nz), jnp.float32)
    plane = pltpu.VMEM((cells, nz), jnp.float32)
    p3, q1, grad = pl.pallas_call(
        functools.partial(kernel, (ndom, nshot)),
        out_shape=(field, field, plane_out),
        in_specs=[hbm] * 5 + [smem] * 4 + [vmem] * 4,
        out_specs=(hbm,) * 3,
        scratch_shapes=[block] * 2
        + [plane]
        + [block] * 3
        + [wide] * 4
        + [pltpu.VMEM((2 * nz, nz), jnp.bfloat16), pltpu.VMEM((rows, 2 * rows), jnp.bfloat16)]
        + [plane] * 5
        + [
            pltpu.SemaphoreType.DMA((5,)),
            pltpu.SemaphoreType.DMA((2 + parts,)),
            pltpu.SemaphoreType.DMA((4, 2)),
            pltpu.SemaphoreType.DMA((4, 2)),
            pltpu.SemaphoreType.DMA((parts, 2 * bits)),
            pltpu.SemaphoreType.DMA((parts, 2 * bits)),
        ],
        compiler_params=pltpu.CompilerParams(
            collective_id=0, has_side_effects=True, vmem_limit_bytes=60 * 1024 * 1024
        ),
        cost_estimate=pl.CostEstimate(flops=4 * 10**9, bytes_accessed=8 * 4 * cells * nz, transcendentals=0),
        name="wave_steps",
    )(
        coefficient,
        fwd_older[0],
        fwd_recent[0],
        adj_later[0],
        adj_recent[0],
        source_xcell,
        source_ycell,
        source_zcell,
        amplitude,
        receiver_xcell,
        receiver_ycell,
        receiver_zcell,
        observed[0],
    )
    p3, q1, grad = pl.pallas_call(
        store_kernel,
        out_shape=(field, field, plane_out),
        in_specs=[hbm] * 3,
        out_specs=(hbm,) * 3,
        scratch_shapes=[block, block, plane, pltpu.SemaphoreType.DMA((2, 2, 3))],
        compiler_params=pltpu.CompilerParams(vmem_limit_bytes=60 * 1024 * 1024),
        cost_estimate=pl.CostEstimate(flops=0, bytes_accessed=6 * 4 * cells * nz, transcendentals=0),
        name="store_results",
    )(p3, q1, grad)
    return p3[None], q1[None], grad.reshape(nx, ny, nz)


def solution(mesh):
    return jax.shard_map(
        shards,
        mesh=mesh,
        in_specs=(
            P("dom", None, None),
            P("shot", "dom", None, None),
            P("shot", "dom", None, None),
            P("shot", "dom", None, None),
            P("shot", "dom", None, None),
            P("shot"),
            P("shot"),
            P("shot"),
            P("shot", None),
            P("shot", None),
            P("shot", None),
            P("shot", None),
            P("shot", None, None),
        ),
        out_specs=(
            P("shot", "dom", None, None),
            P("shot", "dom", None, None),
            P("dom", None, None),
        ),
        check_vma=False,
    )
```

```python
import functools

import jax
import jax.numpy as jnp
from jax import lax
from jax.experimental import pallas as pl
from jax.experimental.pallas import tpu as pltpu
from jax.sharding import PartitionSpec as P

R = 4
CH = 8
MESH = pl.DeviceIdType.MESH
SCALE = 5040.0
W0 = -3.0 * 14350.0
WK = (8064.0, -1008.0, 128.0, -9.0)
P1, Q3, P2, Q2 = range(4)


def band(size, group):
    row = lax.broadcasted_iota(jnp.int32, (size, size), 0)
    col = lax.broadcasted_iota(jnp.int32, (size, size), 1)
    apart = jnp.abs(row - col)
    out = jnp.zeros((size, size), jnp.float32)
    for k, weight in enumerate(WK, 1):
        out = jnp.where(apart == k, weight, out)
    if group < size:
        out = jnp.where(row // group == col // group, out, 0.0)
    return out.astype(jnp.bfloat16)


def kernel(
    dims,
    coef_in,
    older_in,
    recent_in,
    later_in,
    adj_in,
    sx,
    sy,
    sz,
    amp,
    rx,
    ry,
    rz,
    obs,
    out_p3,
    out_q1,
    out_g,
    p3,
    q1,
    gsum,
    coef,
    older,
    later,
    p1,
    q3,
    p2,
    q2,
    zz,
    yy,
    cnt,
    o2,
    o3,
    grad,
    land,
    load,
    save,
    hsend,
    hrecv,
    gsend,
    grecv,
):
    ndom, nshot = dims
    nx, ny, nz = coef.shape
    rows = CH * ny
    npair = nx // CH
    slab = R * ny
    bits = nshot.bit_length() - 1
    parts = gsend.shape[0]
    prow = nx * ny // parts

    dom = lax.axis_index("dom")
    shot = lax.axis_index("shot")
    has_lo = dom > 0
    has_hi = dom < ndom - 1
    bit = [(shot // (1 << b)) % 2 for b in range(bits)]
    partner = [shot + (1 << b) * (1 - 2 * bit[b]) for b in range(bits)]

    own = pl.ds(R, nx)
    loads = [
        pltpu.make_async_copy(src, dst, load.at[i])
        for i, (src, dst) in enumerate(
            (
                (recent_in, p1.at[own]),
                (older_in, older),
                (coef_in, coef),
                (adj_in, q3.at[own]),
                (later_in, later),
            )
        )
    ]
    for copy in loads:
        copy.start()

    barrier = pltpu.get_barrier_semaphore()
    for b in range(bits):
        pl.semaphore_signal(barrier, inc=1, device_id={"shot": partner[b]}, device_id_type=MESH)

    @pl.when(has_lo)
    def _():
        pl.semaphore_signal(barrier, inc=1, device_id={"dom": dom - 1}, device_id_type=MESH)

    @pl.when(has_hi)
    def _():
        pl.semaphore_signal(barrier, inc=1, device_id={"dom": dom + 1}, device_id_type=MESH)

    def down(f, src, first, ref):
        return pltpu.make_async_remote_copy(
            src_ref=src.at[pl.ds(first, R)],
            dst_ref=ref.at[pl.ds(R + nx, R)],
            send_sem=hsend.at[f, 0],
            recv_sem=hrecv.at[f, 1],
            device_id={"dom": dom - 1},
            device_id_type=MESH,
        )

    def up(f, src, first, ref):
        return pltpu.make_async_remote_copy(
            src_ref=src.at[pl.ds(first + nx - R, R)],
            dst_ref=ref.at[pl.ds(0, R)],
            send_sem=hsend.at[f, 1],
            recv_sem=hrecv.at[f, 0],
            device_id={"dom": dom + 1},
            device_id_type=MESH,
        )

    def both(act, f, src, first, ref):
        @pl.when(has_lo)
        def _():
            act(down, up, f, src, first, ref)

        @pl.when(has_hi)
        def _():
            act(up, down, f, src, first, ref)

    def send(*args):
        both(lambda mine, other, *rest: mine(*rest).start(), *args)

    def receive(*args):
        both(lambda mine, other, *rest: other(*rest).wait_recv(), *args)

    def sent(*args):
        both(lambda mine, other, *rest: mine(*rest).wait_send(), *args)

    halo_p1 = (P1, recent_in, 0, p1)
    halo_q3 = (Q3, adj_in, 0, q3)
    halo_p2 = (P2, p2, R, p2)
    halo_q2 = (Q2, q2, R, q2)
    zmat = band(nz, nz)
    zz[0:nz, :] = zmat
    zz[nz : 2 * nz, :] = zmat
    ymat = band(rows, ny)
    yy[:, 0:rows] = ymat
    yy[:, rows : 2 * rows] = ymat

    nothing = jnp.zeros((R, ny, nz), jnp.float32)

    @pl.when(dom == 0)
    def _():
        for ref in (p1, q3, p2, q2):
            ref[0:R] = nothing

    @pl.when(dom == ndom - 1)
    def _():
        for ref in (p1, q3, p2, q2):
            ref[R + nx : R + nx + R] = nothing

    base = dom * nx
    nrecv = rx.shape[1]
    rowid = (rx[...] - base) * ny + ry[...]
    pick = (lax.broadcasted_iota(jnp.int32, (nx * ny, nrecv), 0) == rowid).astype(jnp.float32).astype(jnp.bfloat16)
    onz = lax.broadcasted_iota(jnp.int32, (nz, nrecv), 0) == rz[...]
    nt = (((1,), (1,)), ((), ()))

    def side(values):
        return jnp.where(onz, values, 0.0).astype(jnp.bfloat16)

    sides = [side(1.0)]
    for t in (1, 0):
        value = obs[t : t + 1, :]
        high = value.astype(jnp.bfloat16).astype(jnp.float32)
        sides += [side(high), side(value - high)]
    maps = lax.dot_general(pick, jnp.concatenate(sides, axis=0), nt, preferred_element_type=jnp.float32)
    cnt[...] = maps[:, 0:nz]
    o3[...] = maps[:, nz : 2 * nz] + maps[:, 2 * nz : 3 * nz]
    o2[...] = maps[:, 3 * nz : 4 * nz] + maps[:, 4 * nz : 5 * nz]

    def slabs(c):
        return c * R, nx - R - c * R

    def laplace(refs, c):
        totals, highs, lows = [], [], []
        for ref in refs:
            sides = [ref[pl.ds(first, 3 * R)] for first in slabs(c)]

            def shifted(k):
                return jnp.concatenate([side[R + k : 2 * R + k] for side in sides], axis=0)

            center = shifted(0)
            total = W0 * center
            for k, weight in enumerate(WK, 1):
                total = total + weight * (shifted(k) + shifted(-k))
            totals.append(total.reshape(rows, nz))
            center = center.reshape(rows, nz)
            highs.append(center.astype(jnp.bfloat16))
            lows.append((center - highs[-1].astype(jnp.float32)).astype(jnp.bfloat16))
        high, low = jnp.concatenate(highs, axis=0), jnp.concatenate(lows, axis=0)
        along_z = jnp.dot(jnp.concatenate([high, low], axis=1), zz[...], preferred_element_type=jnp.float32)
        high, low = jnp.concatenate(highs, axis=1), jnp.concatenate(lows, axis=1)
        along_y = jnp.dot(yy[...], jnp.concatenate([high, low], axis=0), preferred_element_type=jnp.float32)
        return [
            (total + (along_z[i * rows : (i + 1) * rows] + along_y[:, i * nz : (i + 1) * nz])) * (1.0 / SCALE)
            for i, total in enumerate(totals)
        ]

    def flat(ref, c, skip=0):
        return jnp.concatenate([ref[pl.ds(skip + first, R)] for first in slabs(c)], axis=0).reshape(rows, nz)

    def put(ref, c, value, skip=0):
        value = value.reshape(CH, ny, nz)
        for i, first in enumerate(slabs(c)):
            ref[pl.ds(skip + first, R)] = value[i * R : (i + 1) * R]

    def slab_rows(first):
        return pl.ds(pl.multiple_of(first * ny, slab), slab)

    def take(ref, c):
        return jnp.concatenate([ref[slab_rows(first), :] for first in slabs(c)], axis=0)

    srow = (sx[0] - base) * ny + sy[0]
    szed = sz[0]

    def source(c, t):
        row = lax.broadcasted_iota(jnp.int32, (rows, 1), 0)
        row = row + jnp.where(row < slab, c * slab, (nx - CH - c * R) * ny)
        lane = lax.broadcasted_iota(jnp.int32, (1, nz), 1)
        return jnp.where(row == srow, amp[0, t], 0.0) * jnp.where(lane == szed, 1.0, 0.0)

    def step_p2(c):
        (change,) = laplace([p1], c)
        value = 2.0 * flat(p1, c, R) - flat(older, c) + flat(coef, c) * (change + source(c, 0))
        put(p2, c, value, R)

    def step_p3_q2(c):
        change_p, change_q = laplace([p2, q3], c)
        scale = flat(coef, c)
        value = 2.0 * flat(p2, c, R) - flat(p1, c, R) + scale * (change_p + source(c, 1))
        put(p3, c, value)
        points = take(cnt, c) * value - take(o3, c)
        value = 2.0 * flat(q3, c, R) - flat(later, c) + scale * (change_q + points)
        put(q2, c, value, R)

    def step_q1(c):
        two = flat(p2, c, R)
        points = take(cnt, c) * two - take(o2, c)
        now = flat(q2, c, R)
        value = 2.0 * now - flat(q3, c, R) + flat(coef, c) * (laplace([q2], c)[0] + points)
        put(q1, c, value)
        one = flat(p1, c, R)
        early = two - 2.0 * one + flat(older, c)
        late = flat(p3, c) - 2.0 * two + one
        term = value * early + now * late
        for i, first in enumerate(slabs(c)):
            grad[slab_rows(first), :] = term[i * slab : (i + 1) * slab]

    def order_of(h):
        order = list(range(bits))
        if h and bits > 1:
            order[0], order[1] = order[1], order[0]
        return order

    def place(p, h, t):
        off = p * prow
        for u, b in enumerate(order_of(h)[:t]):
            off = off + bit[b] * (prow >> (u + 1))
        return off

    def rows_at(off, length):
        return pl.ds(pl.multiple_of(off, 8), length)

    def slot(p, t):
        return rows_at(p * prow + prow - (prow >> t), prow >> (t + 1))

    def reduce_copy(p, h, t):
        b = order_of(h)[t]
        length = prow >> (t + 1)
        give = place(p, h, t) + (1 - bit[b]) * length
        return pltpu.make_async_remote_copy(
            src_ref=grad.at[rows_at(give, length)],
            dst_ref=land.at[slot(p, t)],
            send_sem=gsend.at[p, t],
            recv_sem=grecv.at[p, t],
            device_id={"shot": partner[b]},
            device_id_type=MESH,
        )

    def gather_copy(p, h, t):
        rows_held = rows_at(place(p, h, t + 1), prow >> (t + 1))
        return pltpu.make_async_remote_copy(
            src_ref=gsum.at[rows_held],
            dst_ref=gsum.at[rows_held],
            send_sem=gsend.at[p, bits + t],
            recv_sem=grecv.at[p, bits + t],
            device_id={"shot": partner[order_of(h)[t]]},
            device_id_type=MESH,
        )

    def save_sum(p):
        return pltpu.make_async_copy(gsum.at[rows_at(p * prow, prow)], out_g.at[rows_at(p * prow, prow)], save.at[2 + p])

    def advance(p, h, n):
        if n < bits:
            reduce_copy(p, h, n).wait_recv()
            keep = rows_at(place(p, h, n + 1), prow >> (n + 1))
            total = grad[keep, :] + land[slot(p, n), :]
            if n < bits - 1:
                grad[keep, :] = total
                reduce_copy(p, h, n + 1).start()
            else:
                gsum[keep, :] = total
                gather_copy(p, h, bits - 1).start()
        else:
            t = 2 * bits - 1 - n
            gather_copy(p, h, t).wait_recv()
            if t:
                gather_copy(p, h, t - 1).start()
            else:
                save_sum(p).start()

    early_start = parts == 2 * npair

    def group(c):
        return ((c, 0), (parts - 1 - c, (c + 1) % 2)) if early_start else ((c, c % 2),)

    pl.semaphore_wait(barrier, bits + has_lo.astype(jnp.int32) + has_hi.astype(jnp.int32))
    send(*halo_p1)
    send(*halo_q3)
    for copy in loads[:3]:
        copy.wait()

    def first_turn(i, carry):
        step_p2(npair - 1 - i)
        return carry

    lax.fori_loop(0, npair - 1, first_turn, 0)
    for copy in loads[3:]:
        copy.wait()

    save_p3 = pltpu.make_async_copy(p3, out_p3, save.at[0])
    save_q1 = pltpu.make_async_copy(q1, out_q1, save.at[1])

    def turn(i, carry):
        @pl.when(i == npair - 1)
        def _():
            receive(*halo_p2)

        @pl.when(i < npair)
        def _():
            step_p3_q2(npair - 1 - i)

        @pl.when(i == max(npair - 3, 0))
        def _():
            receive(*halo_p1)
            receive(*halo_q3)
            step_p2(0)
            send(*halo_p2)

        @pl.when(i == npair - 1)
        def _():
            send(*halo_q2)
            save_p3.start()

        @pl.when(i == npair)
        def _():
            receive(*halo_q2)

        @pl.when(i > 0)
        def _():
            step_q1(npair - i)

        if early_start:
            for c in range(npair):

                @pl.when(i == npair - c)
                def _():
                    for p, h in group(c):
                        reduce_copy(p, h, 0).start()

                for n in range(c):

                    @pl.when(i == npair - c + 1 + n)
                    def _():
                        for p, h in group(c):
                            advance(p, h, n)

        return carry

    lax.fori_loop(0, npair + 1, turn, 0)
    save_q1.start()
    steps = 2 * bits
    if early_start:
        left = [(c, c) for c in reversed(range(npair))]
    else:
        left = [(p, 0) for p in range(parts)]
        for p, _ in left:
            for portion in group(p):
                reduce_copy(*portion, 0).start()
    while left:
        for c, n in left:
            for p, h in group(c):
                advance(p, h, n)
        left = [(c, n + 1) for c, n in left if n + 1 < steps]
    for c in range(npair if early_start else parts):
        for p, h in group(c):
            for t in range(bits):
                reduce_copy(p, h, t).wait_send()
                gather_copy(p, h, t).wait_send()
            save_sum(p).wait()
    save_p3.wait()
    save_q1.wait()
    sent(*halo_p1)
    sent(*halo_q3)
    sent(*halo_p2)
    sent(*halo_q2)


def store_kernel(a, b, c, out_a, out_b, out_c, va, vb, vc, sem):
    pieces = 2
    moves = []
    for i in range(pieces):
        for k, (src, mid, dst) in enumerate(((a, va, out_a), (b, vb, out_b), (c, vc, out_c))):
            size = src.shape[0] // pieces
            part = pl.ds(i * size, size)
            come = pltpu.make_async_copy(src.at[part], mid.at[part], sem.at[0, i, k])
            go = pltpu.make_async_copy(mid.at[part], dst.at[part], sem.at[1, i, k])
            come.start()
            moves.append((come, go))
    for come, go in moves:
        come.wait()
        go.start()
    for come, go in moves:
        go.wait()


def shards(
    coefficient,
    fwd_older,
    fwd_recent,
    adj_later,
    adj_recent,
    source_xcell,
    source_ycell,
    source_zcell,
    amplitude,
    receiver_xcell,
    receiver_ycell,
    receiver_zcell,
    observed,
):
    ndom, nshot = lax.axis_size("dom"), lax.axis_size("shot")
    nx, ny, nz = coefficient.shape
    cells = nx * ny
    bits = nshot.bit_length() - 1
    rows = CH * ny
    field = jax.ShapeDtypeStruct((nx, ny, nz), jnp.float32)
    plane_out = jax.ShapeDtypeStruct((cells, nz), jnp.float32)
    parts = 2 * (nx // CH)
    while parts > 1 and (cells // parts) // nshot < 8:
        parts //= 2
    hbm = pl.BlockSpec(memory_space=pltpu.HBM)
    vmem = pl.BlockSpec(memory_space=pltpu.VMEM)
    smem = pl.BlockSpec(memory_space=pltpu.SMEM)
    block = pltpu.VMEM((nx, ny, nz), jnp.float32)
    wide = pltpu.VMEM((nx + 2 * R, ny, nz), jnp.float32)
    plane = pltpu.VMEM((cells, nz), jnp.float32)
    p3, q1, grad = pl.pallas_call(
        functools.partial(kernel, (ndom, nshot)),
        out_shape=(field, field, plane_out),
        in_specs=[hbm] * 5 + [smem] * 4 + [vmem] * 4,
        out_specs=(hbm,) * 3,
        scratch_shapes=[block] * 2
        + [plane]
        + [block] * 3
        + [wide] * 4
        + [pltpu.VMEM((2 * nz, nz), jnp.bfloat16), pltpu.VMEM((rows, 2 * rows), jnp.bfloat16)]
        + [plane] * 5
        + [
            pltpu.SemaphoreType.DMA((5,)),
            pltpu.SemaphoreType.DMA((2 + parts,)),
            pltpu.SemaphoreType.DMA((4, 2)),
            pltpu.SemaphoreType.DMA((4, 2)),
            pltpu.SemaphoreType.DMA((parts, 2 * bits)),
            pltpu.SemaphoreType.DMA((parts, 2 * bits)),
        ],
        compiler_params=pltpu.CompilerParams(
            collective_id=0, has_side_effects=True, vmem_limit_bytes=60 * 1024 * 1024
        ),
        cost_estimate=pl.CostEstimate(flops=4 * 10**9, bytes_accessed=8 * 4 * cells * nz, transcendentals=0),
        name="wave_steps",
    )(
        coefficient,
        fwd_older[0],
        fwd_recent[0],
        adj_later[0],
        adj_recent[0],
        source_xcell,
        source_ycell,
        source_zcell,
        amplitude,
        receiver_xcell,
        receiver_ycell,
        receiver_zcell,
        observed[0],
    )
    p3, q1, grad = pl.pallas_call(
        store_kernel,
        out_shape=(field, field, plane_out),
        in_specs=[hbm] * 3,
        out_specs=(hbm,) * 3,
        scratch_shapes=[block, block, plane, pltpu.SemaphoreType.DMA((2, 2, 3))],
        compiler_params=pltpu.CompilerParams(vmem_limit_bytes=60 * 1024 * 1024),
        cost_estimate=pl.CostEstimate(flops=0, bytes_accessed=6 * 4 * cells * nz, transcendentals=0),
        name="store_results",
    )(p3, q1, grad)
    return p3[None], q1[None], grad.reshape(nx, ny, nz)


def solution(mesh):
    return jax.shard_map(
        shards,
        mesh=mesh,
        in_specs=(
            P("dom", None, None),
            P("shot", "dom", None, None),
            P("shot", "dom", None, None),
            P("shot", "dom", None, None),
            P("shot", "dom", None, None),
            P("shot"),
            P("shot"),
            P("shot"),
            P("shot", None),
            P("shot", None),
            P("shot", None),
            P("shot", None),
            P("shot", None, None),
        ),
        out_specs=(
            P("shot", "dom", None, None),
            P("shot", "dom", None, None),
            P("dom", None, None),
        ),
        check_vma=False,
    )
```

```python
import functools

import jax
import jax.numpy as jnp
from jax import lax
from jax.experimental import pallas as pl
from jax.experimental.pallas import tpu as pltpu
from jax.sharding import PartitionSpec as P

R = 4
CH = 8
MESH = pl.DeviceIdType.MESH
SCALE = 5040.0
W0 = -3.0 * 14350.0
WK = (8064.0, -1008.0, 128.0, -9.0)
P1, Q3, P2, Q2 = range(4)


def band(size, group):
    row = lax.broadcasted_iota(jnp.int32, (size, size), 0)
    col = lax.broadcasted_iota(jnp.int32, (size, size), 1)
    apart = jnp.abs(row - col)
    out = jnp.zeros((size, size), jnp.float32)
    for k, weight in enumerate(WK, 1):
        out = jnp.where(apart == k, weight, out)
    if group < size:
        out = jnp.where(row // group == col // group, out, 0.0)
    return out.astype(jnp.bfloat16)


def kernel(
    dims,
    coef_in,
    older_in,
    recent_in,
    later_in,
    adj_in,
    sx,
    sy,
    sz,
    amp,
    rx,
    ry,
    rz,
    obs,
    p3,
    q1,
    gsum,
    coef,
    older,
    later,
    p1,
    q3,
    p2,
    q2,
    zz,
    yy,
    cnt,
    o2,
    o3,
    grad,
    land,
    load,
    hsend,
    hrecv,
    gsend,
    grecv,
):
    ndom, nshot = dims
    nx, ny, nz = coef.shape
    rows = CH * ny
    npair = nx // CH
    slab = R * ny
    bits = nshot.bit_length() - 1
    parts = gsend.shape[0]
    prow = nx * ny // parts

    dom = lax.axis_index("dom")
    shot = lax.axis_index("shot")
    has_lo = dom > 0
    has_hi = dom < ndom - 1
    bit = [(shot // (1 << b)) % 2 for b in range(bits)]
    partner = [shot + (1 << b) * (1 - 2 * bit[b]) for b in range(bits)]

    own = pl.ds(R, nx)
    loads = [
        pltpu.make_async_copy(src, dst, load.at[i])
        for i, (src, dst) in enumerate(
            (
                (recent_in, p1.at[own]),
                (older_in, older),
                (coef_in, coef),
                (adj_in, q3.at[own]),
                (later_in, later),
            )
        )
    ]
    for copy in loads:
        copy.start()

    barrier = pltpu.get_barrier_semaphore()
    for b in range(bits):
        pl.semaphore_signal(barrier, inc=1, device_id={"shot": partner[b]}, device_id_type=MESH)

    @pl.when(has_lo)
    def _():
        pl.semaphore_signal(barrier, inc=1, device_id={"dom": dom - 1}, device_id_type=MESH)

    @pl.when(has_hi)
    def _():
        pl.semaphore_signal(barrier, inc=1, device_id={"dom": dom + 1}, device_id_type=MESH)

    def down(f, src, first, ref):
        return pltpu.make_async_remote_copy(
            src_ref=src.at[pl.ds(first, R)],
            dst_ref=ref.at[pl.ds(R + nx, R)],
            send_sem=hsend.at[f, 0],
            recv_sem=hrecv.at[f, 1],
            device_id={"dom": dom - 1},
            device_id_type=MESH,
        )

    def up(f, src, first, ref):
        return pltpu.make_async_remote_copy(
            src_ref=src.at[pl.ds(first + nx - R, R)],
            dst_ref=ref.at[pl.ds(0, R)],
            send_sem=hsend.at[f, 1],
            recv_sem=hrecv.at[f, 0],
            device_id={"dom": dom + 1},
            device_id_type=MESH,
        )

    def both(act, f, src, first, ref):
        @pl.when(has_lo)
        def _():
            act(down, up, f, src, first, ref)

        @pl.when(has_hi)
        def _():
            act(up, down, f, src, first, ref)

    def send(*args):
        both(lambda mine, other, *rest: mine(*rest).start(), *args)

    def receive(*args):
        both(lambda mine, other, *rest: other(*rest).wait_recv(), *args)

    def sent(*args):
        both(lambda mine, other, *rest: mine(*rest).wait_send(), *args)

    halo_p1 = (P1, recent_in, 0, p1)
    halo_q3 = (Q3, adj_in, 0, q3)
    halo_p2 = (P2, p2, R, p2)
    halo_q2 = (Q2, q2, R, q2)
    zmat = band(nz, nz)
    zz[0:nz, :] = zmat
    zz[nz : 2 * nz, :] = zmat
    ymat = band(rows, ny)
    yy[:, 0:rows] = ymat
    yy[:, rows : 2 * rows] = ymat

    nothing = jnp.zeros((R, ny, nz), jnp.float32)

    @pl.when(dom == 0)
    def _():
        for ref in (p1, q3, p2, q2):
            ref[0:R] = nothing

    @pl.when(dom == ndom - 1)
    def _():
        for ref in (p1, q3, p2, q2):
            ref[R + nx : R + nx + R] = nothing

    base = dom * nx
    nrecv = rx.shape[1]
    rowid = (rx[...] - base) * ny + ry[...]
    pick = (lax.broadcasted_iota(jnp.int32, (nx * ny, nrecv), 0) == rowid).astype(jnp.float32).astype(jnp.bfloat16)
    onz = lax.broadcasted_iota(jnp.int32, (nz, nrecv), 0) == rz[...]
    nt = (((1,), (1,)), ((), ()))

    def side(values):
        return jnp.where(onz, values, 0.0).astype(jnp.bfloat16)

    sides = [side(1.0)]
    for t in (1, 0):
        value = obs[t : t + 1, :]
        high = value.astype(jnp.bfloat16).astype(jnp.float32)
        sides += [side(high), side(value - high)]
    maps = lax.dot_general(pick, jnp.concatenate(sides, axis=0), nt, preferred_element_type=jnp.float32)
    cnt[...] = maps[:, 0:nz]
    o3[...] = maps[:, nz : 2 * nz] + maps[:, 2 * nz : 3 * nz]
    o2[...] = maps[:, 3 * nz : 4 * nz] + maps[:, 4 * nz : 5 * nz]

    def slabs(c):
        return c * R, nx - R - c * R

    def laplace(refs, c):
        totals, highs, lows = [], [], []
        for ref in refs:
            sides = [ref[pl.ds(first, 3 * R)] for first in slabs(c)]

            def shifted(k):
                return jnp.concatenate([side[R + k : 2 * R + k] for side in sides], axis=0)

            center = shifted(0)
            total = W0 * center
            for k, weight in enumerate(WK, 1):
                total = total + weight * (shifted(k) + shifted(-k))
            totals.append(total.reshape(rows, nz))
            center = center.reshape(rows, nz)
            highs.append(center.astype(jnp.bfloat16))
            lows.append((center - highs[-1].astype(jnp.float32)).astype(jnp.bfloat16))
        high, low = jnp.concatenate(highs, axis=0), jnp.concatenate(lows, axis=0)
        along_z = jnp.dot(jnp.concatenate([high, low], axis=1), zz[...], preferred_element_type=jnp.float32)
        high, low = jnp.concatenate(highs, axis=1), jnp.concatenate(lows, axis=1)
        along_y = jnp.dot(yy[...], jnp.concatenate([high, low], axis=0), preferred_element_type=jnp.float32)
        return [
            (total + (along_z[i * rows : (i + 1) * rows] + along_y[:, i * nz : (i + 1) * nz])) * (1.0 / SCALE)
            for i, total in enumerate(totals)
        ]

    def flat(ref, c, skip=0):
        return jnp.concatenate([ref[pl.ds(skip + first, R)] for first in slabs(c)], axis=0).reshape(rows, nz)

    def put(ref, c, value, skip=0):
        value = value.reshape(CH, ny, nz)
        for i, first in enumerate(slabs(c)):
            ref[pl.ds(skip + first, R)] = value[i * R : (i + 1) * R]

    def slab_rows(first):
        return pl.ds(pl.multiple_of(first * ny, slab), slab)

    def take(ref, c):
        return jnp.concatenate([ref[slab_rows(first), :] for first in slabs(c)], axis=0)

    srow = (sx[0] - base) * ny + sy[0]
    szed = sz[0]

    def source(c, t):
        row = lax.broadcasted_iota(jnp.int32, (rows, 1), 0)
        row = row + jnp.where(row < slab, c * slab, (nx - CH - c * R) * ny)
        lane = lax.broadcasted_iota(jnp.int32, (1, nz), 1)
        return jnp.where(row == srow, amp[0, t], 0.0) * jnp.where(lane == szed, 1.0, 0.0)

    def step_p2(c):
        (change,) = laplace([p1], c)
        value = 2.0 * flat(p1, c, R) - flat(older, c) + flat(coef, c) * (change + source(c, 0))
        put(p2, c, value, R)

    def step_p3_q2(c):
        change_p, change_q = laplace([p2, q3], c)
        scale = flat(coef, c)
        value = 2.0 * flat(p2, c, R) - flat(p1, c, R) + scale * (change_p + source(c, 1))
        put(p3, c, value)
        points = take(cnt, c) * value - take(o3, c)
        value = 2.0 * flat(q3, c, R) - flat(later, c) + scale * (change_q + points)
        put(q2, c, value, R)

    def step_q1(c):
        two = flat(p2, c, R)
        points = take(cnt, c) * two - take(o2, c)
        now = flat(q2, c, R)
        value = 2.0 * now - flat(q3, c, R) + flat(coef, c) * (laplace([q2], c)[0] + points)
        put(q1, c, value)
        one = flat(p1, c, R)
        early = two - 2.0 * one + flat(older, c)
        late = flat(p3, c) - 2.0 * two + one
        term = value * early + now * late
        grad[pl.ds(pl.multiple_of(c * rows, rows), rows), :] = term

    def order_of(h):
        order = list(range(bits))
        if h and bits > 1:
            order[0], order[1] = order[1], order[0]
        return order

    def place(p, h, t):
        off = p * prow
        for u, b in enumerate(order_of(h)[:t]):
            off = off + bit[b] * (prow >> (u + 1))
        return off

    def rows_at(off, length):
        return pl.ds(pl.multiple_of(off, 8), length)

    def slot(p, t):
        return rows_at(p * prow + prow - (prow >> t), prow >> (t + 1))

    def reduce_copy(p, h, t):
        b = order_of(h)[t]
        length = prow >> (t + 1)
        give = place(p, h, t) + (1 - bit[b]) * length
        return pltpu.make_async_remote_copy(
            src_ref=grad.at[rows_at(give, length)],
            dst_ref=land.at[slot(p, t)],
            send_sem=gsend.at[p, t],
            recv_sem=grecv.at[p, t],
            device_id={"shot": partner[b]},
            device_id_type=MESH,
        )

    def gather_copy(p, h, t):
        rows_held = rows_at(place(p, h, t + 1), prow >> (t + 1))
        return pltpu.make_async_remote_copy(
            src_ref=gsum.at[rows_held],
            dst_ref=gsum.at[rows_held],
            send_sem=gsend.at[p, bits + t],
            recv_sem=grecv.at[p, bits + t],
            device_id={"shot": partner[order_of(h)[t]]},
            device_id_type=MESH,
        )

    def advance(p, h, n):
        if n < bits:
            reduce_copy(p, h, n).wait_recv()
            keep = rows_at(place(p, h, n + 1), prow >> (n + 1))
            total = grad[keep, :] + land[slot(p, n), :]
            if n < bits - 1:
                grad[keep, :] = total
                reduce_copy(p, h, n + 1).start()
            else:
                gsum[keep, :] = total
                gather_copy(p, h, bits - 1).start()
        else:
            t = 2 * bits - 1 - n
            gather_copy(p, h, t).wait_recv()
            if t:
                gather_copy(p, h, t - 1).start()

    early_start = parts == npair

    def group(c):
        return ((c, (c + 1) % 2),)

    pl.semaphore_wait(barrier, bits + has_lo.astype(jnp.int32) + has_hi.astype(jnp.int32))
    send(*halo_p1)
    send(*halo_q3)
    for copy in loads[:3]:
        copy.wait()

    def first_turn(i, carry):
        step_p2(npair - 1 - i)
        return carry

    lax.fori_loop(0, npair - 1, first_turn, 0)
    for copy in loads[3:]:
        copy.wait()

    def turn(i, carry):
        @pl.when(i == npair - 1)
        def _():
            receive(*halo_p2)

        @pl.when(i < npair)
        def _():
            step_p3_q2(npair - 1 - i)

        @pl.when(i == max(npair - 3, 0))
        def _():
            receive(*halo_p1)
            receive(*halo_q3)
            step_p2(0)
            send(*halo_p2)

        @pl.when(i == npair - 1)
        def _():
            send(*halo_q2)

        @pl.when(i == npair)
        def _():
            receive(*halo_q2)

        @pl.when(i > 0)
        def _():
            step_q1(npair - i)

        if early_start:
            for c in range(npair):

                @pl.when(i == npair - c)
                def _():
                    for p, h in group(c):
                        reduce_copy(p, h, 0).start()

                for n in range(c):

                    @pl.when(i == npair - c + 1 + n)
                    def _():
                        for p, h in group(c):
                            advance(p, h, n)

        return carry

    lax.fori_loop(0, npair + 1, turn, 0)
    steps = 2 * bits
    if early_start:
        left = [(c, c) for c in reversed(range(npair))]
    else:
        left = [(p, 0) for p in range(parts)]
        for p, _ in left:
            for portion in group(p):
                reduce_copy(*portion, 0).start()
    while left:
        for c, n in left:
            for p, h in group(c):
                advance(p, h, n)
        left = [(c, n + 1) for c, n in left if n + 1 < steps]
    for c in range(npair if early_start else parts):
        for p, h in group(c):
            for t in range(bits):
                reduce_copy(p, h, t).wait_send()
                gather_copy(p, h, t).wait_send()
    sent(*halo_p1)
    sent(*halo_q3)
    sent(*halo_p2)
    sent(*halo_q2)


def store_kernel(a, b, c, out_a, out_b, out_c, sem):
    moves = [(a, out_a), (b, out_b)]
    slab = R * out_a.shape[1]
    count = c.shape[0] // slab
    for i in range(count):
        to = i // 2 if i % 2 == 0 else count - 1 - i // 2
        moves.append((c.at[pl.ds(i * slab, slab)], out_c.at[pl.ds(to * slab, slab)]))
    copies = [pltpu.make_async_copy(src, dst, sem.at[i]) for i, (src, dst) in enumerate(moves)]
    for copy in copies:
        copy.start()
    for copy in copies:
        copy.wait()


def shards(
    coefficient,
    fwd_older,
    fwd_recent,
    adj_later,
    adj_recent,
    source_xcell,
    source_ycell,
    source_zcell,
    amplitude,
    receiver_xcell,
    receiver_ycell,
    receiver_zcell,
    observed,
):
    ndom, nshot = lax.axis_size("dom"), lax.axis_size("shot")
    nx, ny, nz = coefficient.shape
    cells = nx * ny
    bits = nshot.bit_length() - 1
    rows = CH * ny
    field = jax.ShapeDtypeStruct((nx, ny, nz), jnp.float32)
    plane_out = jax.ShapeDtypeStruct((cells, nz), jnp.float32)
    parts = nx // CH
    while parts > 1 and (cells // parts) // nshot < 8:
        parts //= 2
    hbm = pl.BlockSpec(memory_space=pltpu.HBM)
    vmem = pl.BlockSpec(memory_space=pltpu.VMEM)
    smem = pl.BlockSpec(memory_space=pltpu.SMEM)
    block = pltpu.VMEM((nx, ny, nz), jnp.float32)
    wide = pltpu.VMEM((nx + 2 * R, ny, nz), jnp.float32)
    plane = pltpu.VMEM((cells, nz), jnp.float32)
    p3, q1, grad = pl.pallas_call(
        functools.partial(kernel, (ndom, nshot)),
        out_shape=(field, field, plane_out),
        in_specs=[hbm] * 5 + [smem] * 4 + [vmem] * 4,
        out_specs=(vmem,) * 3,
        scratch_shapes=[block] * 3
        + [wide] * 4
        + [pltpu.VMEM((2 * nz, nz), jnp.bfloat16), pltpu.VMEM((rows, 2 * rows), jnp.bfloat16)]
        + [plane] * 5
        + [
            pltpu.SemaphoreType.DMA((5,)),
            pltpu.SemaphoreType.DMA((4, 2)),
            pltpu.SemaphoreType.DMA((4, 2)),
            pltpu.SemaphoreType.DMA((parts, 2 * bits)),
            pltpu.SemaphoreType.DMA((parts, 2 * bits)),
        ],
        compiler_params=pltpu.CompilerParams(
            collective_id=0, has_side_effects=True, vmem_limit_bytes=51 * 1024 * 1024
        ),
        cost_estimate=pl.CostEstimate(flops=4 * 10**9, bytes_accessed=8 * 4 * cells * nz, transcendentals=0),
        name="wave_steps",
    )(
        coefficient,
        fwd_older[0],
        fwd_recent[0],
        adj_later[0],
        adj_recent[0],
        source_xcell,
        source_ycell,
        source_zcell,
        amplitude,
        receiver_xcell,
        receiver_ycell,
        receiver_zcell,
        observed[0],
    )
    p3, q1, grad = pl.pallas_call(
        store_kernel,
        out_shape=(field, field, plane_out),
        in_specs=[vmem] * 3,
        out_specs=(hbm,) * 3,
        scratch_shapes=[pltpu.SemaphoreType.DMA((2 + nx // R,))],
        compiler_params=pltpu.CompilerParams(vmem_limit_bytes=16 * 1024 * 1024),
        cost_estimate=pl.CostEstimate(flops=0, bytes_accessed=6 * 4 * cells * nz, transcendentals=0),
        name="store_results",
    )(p3, q1, grad)
    return p3[None], q1[None], grad.reshape(nx, ny, nz)


def solution(mesh):
    return jax.shard_map(
        shards,
        mesh=mesh,
        in_specs=(
            P("dom", None, None),
            P("shot", "dom", None, None),
            P("shot", "dom", None, None),
            P("shot", "dom", None, None),
            P("shot", "dom", None, None),
            P("shot"),
            P("shot"),
            P("shot"),
            P("shot", None),
            P("shot", None),
            P("shot", None),
            P("shot", None),
            P("shot", None, None),
        ),
        out_specs=(
            P("shot", "dom", None, None),
            P("shot", "dom", None, None),
            P("dom", None, None),
        ),
        check_vma=False,
    )
```

```python
import functools

import jax
import jax.numpy as jnp
from jax import lax
from jax.experimental import pallas as pl
from jax.experimental.pallas import tpu as pltpu
from jax.sharding import PartitionSpec as P

R = 4
CH = 8
MESH = pl.DeviceIdType.MESH
SCALE = 5040.0
W0 = -3.0 * 14350.0
WK = (8064.0, -1008.0, 128.0, -9.0)
P1, Q3, P2, Q2 = range(4)


def band(size, group):
    row = lax.broadcasted_iota(jnp.int32, (size, size), 0)
    col = lax.broadcasted_iota(jnp.int32, (size, size), 1)
    apart = jnp.abs(row - col)
    out = jnp.zeros((size, size), jnp.float32)
    for k, weight in enumerate(WK, 1):
        out = jnp.where(apart == k, weight, out)
    if group < size:
        out = jnp.where(row // group == col // group, out, 0.0)
    return out.astype(jnp.bfloat16)


def kernel(
    dims,
    coef_in,
    older_in,
    recent_in,
    later_in,
    adj_in,
    sx,
    sy,
    sz,
    amp,
    rx,
    ry,
    rz,
    obs,
    out_p3,
    out_q1,
    out_g,
    p3,
    q1,
    gsum,
    coef,
    older,
    later,
    p1,
    q3,
    p2,
    q2,
    zz,
    yy,
    cnt,
    o2,
    o3,
    grad,
    land,
    load,
    save,
    hsend,
    hrecv,
    gsend,
    grecv,
):
    ndom, nshot = dims
    nx, ny, nz = coef.shape
    rows = CH * ny
    npair = nx // CH
    slab = R * ny
    bits = nshot.bit_length() - 1
    parts = gsend.shape[0]
    prow = nx * ny // parts

    dom = lax.axis_index("dom")
    shot = lax.axis_index("shot")
    has_lo = dom > 0
    has_hi = dom < ndom - 1
    bit = [(shot // (1 << b)) % 2 for b in range(bits)]
    partner = [shot + (1 << b) * (1 - 2 * bit[b]) for b in range(bits)]

    own = pl.ds(R, nx)
    loads = [
        pltpu.make_async_copy(src, dst, load.at[i])
        for i, (src, dst) in enumerate(
            (
                (recent_in, p1.at[own]),
                (older_in, older),
                (coef_in, coef),
                (adj_in, q3.at[own]),
                (later_in, later),
            )
        )
    ]
    for copy in loads:
        copy.start()

    barrier = pltpu.get_barrier_semaphore()
    for b in range(bits):
        pl.semaphore_signal(barrier, inc=1, device_id={"shot": partner[b]}, device_id_type=MESH)

    @pl.when(has_lo)
    def _():
        pl.semaphore_signal(barrier, inc=1, device_id={"dom": dom - 1}, device_id_type=MESH)

    @pl.when(has_hi)
    def _():
        pl.semaphore_signal(barrier, inc=1, device_id={"dom": dom + 1}, device_id_type=MESH)

    def down(f, src, first, ref):
        return pltpu.make_async_remote_copy(
            src_ref=src.at[pl.ds(first, R)],
            dst_ref=ref.at[pl.ds(R + nx, R)],
            send_sem=hsend.at[f, 0],
            recv_sem=hrecv.at[f, 1],
            device_id={"dom": dom - 1},
            device_id_type=MESH,
        )

    def up(f, src, first, ref):
        return pltpu.make_async_remote_copy(
            src_ref=src.at[pl.ds(first + nx - R, R)],
            dst_ref=ref.at[pl.ds(0, R)],
            send_sem=hsend.at[f, 1],
            recv_sem=hrecv.at[f, 0],
            device_id={"dom": dom + 1},
            device_id_type=MESH,
        )

    def both(act, f, src, first, ref):
        @pl.when(has_lo)
        def _():
            act(down, up, f, src, first, ref)

        @pl.when(has_hi)
        def _():
            act(up, down, f, src, first, ref)

    def send(*args):
        both(lambda mine, other, *rest: mine(*rest).start(), *args)

    def receive(*args):
        both(lambda mine, other, *rest: other(*rest).wait_recv(), *args)

    def sent(*args):
        both(lambda mine, other, *rest: mine(*rest).wait_send(), *args)

    halo_p1 = (P1, recent_in, 0, p1)
    halo_q3 = (Q3, adj_in, 0, q3)
    halo_p2 = (P2, p2, R, p2)
    halo_q2 = (Q2, q2, R, q2)
    zmat = band(nz, nz)
    zz[0:nz, :] = zmat
    zz[nz : 2 * nz, :] = zmat
    ymat = band(rows, ny)
    yy[:, 0:rows] = ymat
    yy[:, rows : 2 * rows] = ymat

    nothing = jnp.zeros((R, ny, nz), jnp.float32)

    @pl.when(dom == 0)
    def _():
        for ref in (p1, q3, p2, q2):
            ref[0:R] = nothing

    @pl.when(dom == ndom - 1)
    def _():
        for ref in (p1, q3, p2, q2):
            ref[R + nx : R + nx + R] = nothing

    base = dom * nx
    nrecv = rx.shape[1]
    rowid = (rx[...] - base) * ny + ry[...]
    pick = (lax.broadcasted_iota(jnp.int32, (nx * ny, nrecv), 0) == rowid).astype(jnp.float32).astype(jnp.bfloat16)
    onz = lax.broadcasted_iota(jnp.int32, (nz, nrecv), 0) == rz[...]
    nt = (((1,), (1,)), ((), ()))

    def side(values):
        return jnp.where(onz, values, 0.0).astype(jnp.bfloat16)

    sides = [side(1.0)]
    for t in (1, 0):
        value = obs[t : t + 1, :]
        high = value.astype(jnp.bfloat16).astype(jnp.float32)
        sides += [side(high), side(value - high)]
    maps = lax.dot_general(pick, jnp.concatenate(sides, axis=0), nt, preferred_element_type=jnp.float32)
    cnt[...] = maps[:, 0:nz]
    o3[...] = maps[:, nz : 2 * nz] + maps[:, 2 * nz : 3 * nz]
    o2[...] = maps[:, 3 * nz : 4 * nz] + maps[:, 4 * nz : 5 * nz]

    def slabs(c):
        return c * R, nx - R - c * R

    def laplace(refs, c):
        totals, highs, lows = [], [], []
        for ref in refs:
            sides = [ref[pl.ds(first, 3 * R)] for first in slabs(c)]

            def shifted(k):
                return jnp.concatenate([side[R + k : 2 * R + k] for side in sides], axis=0)

            center = shifted(0)
            total = W0 * center
            for k, weight in enumerate(WK, 1):
                total = total + weight * (shifted(k) + shifted(-k))
            totals.append(total.reshape(rows, nz))
            center = center.reshape(rows, nz)
            highs.append(center.astype(jnp.bfloat16))
            lows.append((center - highs[-1].astype(jnp.float32)).astype(jnp.bfloat16))
        high, low = jnp.concatenate(highs, axis=0), jnp.concatenate(lows, axis=0)
        along_z = jnp.dot(jnp.concatenate([high, low], axis=1), zz[...], preferred_element_type=jnp.float32)
        high, low = jnp.concatenate(highs, axis=1), jnp.concatenate(lows, axis=1)
        along_y = jnp.dot(yy[...], jnp.concatenate([high, low], axis=0), preferred_element_type=jnp.float32)
        return [
            (total + (along_z[i * rows : (i + 1) * rows] + along_y[:, i * nz : (i + 1) * nz])) * (1.0 / SCALE)
            for i, total in enumerate(totals)
        ]

    def flat(ref, c, skip=0):
        return jnp.concatenate([ref[pl.ds(skip + first, R)] for first in slabs(c)], axis=0).reshape(rows, nz)

    def put(ref, c, value, skip=0):
        value = value.reshape(CH, ny, nz)
        for i, first in enumerate(slabs(c)):
            ref[pl.ds(skip + first, R)] = value[i * R : (i + 1) * R]

    def slab_rows(first):
        return pl.ds(pl.multiple_of(first * ny, slab), slab)

    def take(ref, c):
        return jnp.concatenate([ref[slab_rows(first), :] for first in slabs(c)], axis=0)

    srow = (sx[0] - base) * ny + sy[0]
    szed = sz[0]

    def source(c, t):
        row = lax.broadcasted_iota(jnp.int32, (rows, 1), 0)
        row = row + jnp.where(row < slab, c * slab, (nx - CH - c * R) * ny)
        lane = lax.broadcasted_iota(jnp.int32, (1, nz), 1)
        return jnp.where(row == srow, amp[0, t], 0.0) * jnp.where(lane == szed, 1.0, 0.0)

    def step_p2(c):
        (change,) = laplace([p1], c)
        value = 2.0 * flat(p1, c, R) - flat(older, c) + flat(coef, c) * (change + source(c, 0))
        put(p2, c, value, R)

    def step_p3_q2(c):
        change_p, change_q = laplace([p2, q3], c)
        scale = flat(coef, c)
        value = 2.0 * flat(p2, c, R) - flat(p1, c, R) + scale * (change_p + source(c, 1))
        put(p3, c, value)
        points = take(cnt, c) * value - take(o3, c)
        value = 2.0 * flat(q3, c, R) - flat(later, c) + scale * (change_q + points)
        put(q2, c, value, R)

    def step_q1(c):
        two = flat(p2, c, R)
        points = take(cnt, c) * two - take(o2, c)
        now = flat(q2, c, R)
        value = 2.0 * now - flat(q3, c, R) + flat(coef, c) * (laplace([q2], c)[0] + points)
        put(q1, c, value)
        one = flat(p1, c, R)
        early = two - 2.0 * one + flat(older, c)
        late = flat(p3, c) - 2.0 * two + one
        term = value * early + now * late
        for i, first in enumerate(slabs(c)):
            grad[slab_rows(first), :] = term[i * slab : (i + 1) * slab]

    def order_of(h):
        order = list(range(bits))
        if h and bits > 1:
            order[0], order[1] = order[1], order[0]
        return order

    def place(p, h, t):
        off = p * prow
        for u, b in enumerate(order_of(h)[:t]):
            off = off + bit[b] * (prow >> (u + 1))
        return off

    def rows_at(off, length):
        return pl.ds(pl.multiple_of(off, 8), length)

    def slot(p, t):
        return rows_at(p * prow + prow - (prow >> t), prow >> (t + 1))

    def reduce_copy(p, h, t):
        b = order_of(h)[t]
        length = prow >> (t + 1)
        give = place(p, h, t) + (1 - bit[b]) * length
        return pltpu.make_async_remote_copy(
            src_ref=grad.at[rows_at(give, length)],
            dst_ref=land.at[slot(p, t)],
            send_sem=gsend.at[p, t],
            recv_sem=grecv.at[p, t],
            device_id={"shot": partner[b]},
            device_id_type=MESH,
        )

    def gather_copy(p, h, t):
        rows_held = rows_at(place(p, h, t + 1), prow >> (t + 1))
        return pltpu.make_async_remote_copy(
            src_ref=gsum.at[rows_held],
            dst_ref=gsum.at[rows_held],
            send_sem=gsend.at[p, bits + t],
            recv_sem=grecv.at[p, bits + t],
            device_id={"shot": partner[order_of(h)[t]]},
            device_id_type=MESH,
        )

    def save_sum(p):
        return pltpu.make_async_copy(gsum.at[rows_at(p * prow, prow)], out_g.at[rows_at(p * prow, prow)], save.at[2 + p])

    def advance(p, h, n):
        if n < bits:
            reduce_copy(p, h, n).wait_recv()
            keep = rows_at(place(p, h, n + 1), prow >> (n + 1))
            total = grad[keep, :] + land[slot(p, n), :]
            if n < bits - 1:
                grad[keep, :] = total
                reduce_copy(p, h, n + 1).start()
            else:
                gsum[keep, :] = total
                gather_copy(p, h, bits - 1).start()
        else:
            t = 2 * bits - 1 - n
            gather_copy(p, h, t).wait_recv()
            if t:
                gather_copy(p, h, t - 1).start()
            else:
                save_sum(p).start()

    early_start = parts == 2 * npair

    def group(c):
        return ((c, 0), (parts - 1 - c, (c + 1) % 2)) if early_start else ((c, c % 2),)

    pl.semaphore_wait(barrier, bits + has_lo.astype(jnp.int32) + has_hi.astype(jnp.int32))
    send(*halo_p1)
    send(*halo_q3)
    for copy in loads[:3]:
        copy.wait()

    def first_turn(i, carry):
        step_p2(npair - 1 - i)
        return carry

    lax.fori_loop(0, npair - 1, first_turn, 0)
    for copy in loads[3:]:
        copy.wait()

    save_p3 = pltpu.make_async_copy(p3, out_p3, save.at[0])
    save_q1 = pltpu.make_async_copy(q1, out_q1, save.at[1])

    def turn(i, carry):
        @pl.when(i == npair - 1)
        def _():
            receive(*halo_p2)

        @pl.when(i < npair)
        def _():
            step_p3_q2(npair - 1 - i)

        @pl.when(i == max(npair - 3, 0))
        def _():
            receive(*halo_p1)
            receive(*halo_q3)
            step_p2(0)
            send(*halo_p2)

        @pl.when(i == npair - 1)
        def _():
            send(*halo_q2)
            save_p3.start()

        @pl.when(i == npair)
        def _():
            receive(*halo_q2)

        @pl.when(i > 0)
        def _():
            step_q1(npair - i)

        if early_start:
            for c in range(npair):

                @pl.when(i == npair - c)
                def _():
                    for p, h in group(c):
                        reduce_copy(p, h, 0).start()

                for n in range(c - 1):

                    @pl.when(i == npair - c + 2 + n)
                    def _():
                        for p, h in group(c):
                            advance(p, h, n)

        return carry

    lax.fori_loop(0, npair + 1, turn, 0)
    save_q1.start()
    steps = 2 * bits
    if early_start:
        left = [(c, max(c - 1, 0)) for c in reversed(range(npair))]
    else:
        left = [(p, 0) for p in range(parts)]
        for p, _ in left:
            for portion in group(p):
                reduce_copy(*portion, 0).start()
    while left:
        for c, n in left:
            for p, h in group(c):
                advance(p, h, n)
        left = [(c, n + 1) for c, n in left if n + 1 < steps]
    for c in range(npair if early_start else parts):
        for p, h in group(c):
            for t in range(bits):
                reduce_copy(p, h, t).wait_send()
                gather_copy(p, h, t).wait_send()
            save_sum(p).wait()
    save_p3.wait()
    save_q1.wait()
    sent(*halo_p1)
    sent(*halo_q3)
    sent(*halo_p2)
    sent(*halo_q2)


def store_kernel(a, b, c, out_a, out_b, out_c, va, vb, vc, sem):
    pieces = 4
    moves = []
    for i in range(pieces):
        for k, (src, mid, dst) in enumerate(((a, va, out_a), (b, vb, out_b), (c, vc, out_c))):
            size = src.shape[0] // pieces
            part = pl.ds(i * size, size)
            come = pltpu.make_async_copy(src.at[part], mid.at[part], sem.at[0, i, k])
            go = pltpu.make_async_copy(mid.at[part], dst.at[part], sem.at[1, i, k])
            come.start()
            moves.append((come, go))
    for come, go in moves:
        come.wait()
        go.start()
    for come, go in moves:
        go.wait()


def shards(
    coefficient,
    fwd_older,
    fwd_recent,
    adj_later,
    adj_recent,
    source_xcell,
    source_ycell,
    source_zcell,
    amplitude,
    receiver_xcell,
    receiver_ycell,
    receiver_zcell,
    observed,
):
    ndom, nshot = lax.axis_size("dom"), lax.axis_size("shot")
    nx, ny, nz = coefficient.shape
    cells = nx * ny
    bits = nshot.bit_length() - 1
    rows = CH * ny
    field = jax.ShapeDtypeStruct((nx, ny, nz), jnp.float32)
    plane_out = jax.ShapeDtypeStruct((cells, nz), jnp.float32)
    parts = 2 * (nx // CH)
    while parts > 1 and (cells // parts) // nshot < 8:
        parts //= 2
    hbm = pl.BlockSpec(memory_space=pltpu.HBM)
    vmem = pl.BlockSpec(memory_space=pltpu.VMEM)
    smem = pl.BlockSpec(memory_space=pltpu.SMEM)
    block = pltpu.VMEM((nx, ny, nz), jnp.float32)
    wide = pltpu.VMEM((nx + 2 * R, ny, nz), jnp.float32)
    plane = pltpu.VMEM((cells, nz), jnp.float32)
    p3, q1, grad = pl.pallas_call(
        functools.partial(kernel, (ndom, nshot)),
        out_shape=(field, field, plane_out),
        in_specs=[hbm] * 5 + [smem] * 4 + [vmem] * 4,
        out_specs=(hbm,) * 3,
        scratch_shapes=[block] * 2
        + [plane]
        + [block] * 3
        + [wide] * 4
        + [pltpu.VMEM((2 * nz, nz), jnp.bfloat16), pltpu.VMEM((rows, 2 * rows), jnp.bfloat16)]
        + [plane] * 5
        + [
            pltpu.SemaphoreType.DMA((5,)),
            pltpu.SemaphoreType.DMA((2 + parts,)),
            pltpu.SemaphoreType.DMA((4, 2)),
            pltpu.SemaphoreType.DMA((4, 2)),
            pltpu.SemaphoreType.DMA((parts, 2 * bits)),
            pltpu.SemaphoreType.DMA((parts, 2 * bits)),
        ],
        compiler_params=pltpu.CompilerParams(
            collective_id=0, has_side_effects=True, vmem_limit_bytes=60 * 1024 * 1024
        ),
        cost_estimate=pl.CostEstimate(flops=4 * 10**9, bytes_accessed=8 * 4 * cells * nz, transcendentals=0),
        name="wave_steps",
    )(
        coefficient,
        fwd_older[0],
        fwd_recent[0],
        adj_later[0],
        adj_recent[0],
        source_xcell,
        source_ycell,
        source_zcell,
        amplitude,
        receiver_xcell,
        receiver_ycell,
        receiver_zcell,
        observed[0],
    )
    p3, q1, grad = pl.pallas_call(
        store_kernel,
        out_shape=(field, field, plane_out),
        in_specs=[hbm] * 3,
        out_specs=(hbm,) * 3,
        scratch_shapes=[block, block, plane, pltpu.SemaphoreType.DMA((2, 4, 3))],
        compiler_params=pltpu.CompilerParams(vmem_limit_bytes=60 * 1024 * 1024),
        cost_estimate=pl.CostEstimate(flops=0, bytes_accessed=6 * 4 * cells * nz, transcendentals=0),
        name="store_results",
    )(p3, q1, grad)
    return p3[None], q1[None], grad.reshape(nx, ny, nz)


def solution(mesh):
    return jax.shard_map(
        shards,
        mesh=mesh,
        in_specs=(
            P("dom", None, None),
            P("shot", "dom", None, None),
            P("shot", "dom", None, None),
            P("shot", "dom", None, None),
            P("shot", "dom", None, None),
            P("shot"),
            P("shot"),
            P("shot"),
            P("shot", None),
            P("shot", None),
            P("shot", None),
            P("shot", None),
            P("shot", None, None),
        ),
        out_specs=(
            P("shot", "dom", None, None),
            P("shot", "dom", None, None),
            P("dom", None, None),
        ),
        check_vma=False,
    )
```
